32 devices in a mesh: groups: 2 (over x), seq: 8 (over z, y), expert: 2 (over core).
Axes of the slice: x: 2, y: 2, z: 4, core: 2. Of those that a mesh axis runs over, the one named last changes fastest.
Arguments:
- queries: bfloat16 [4, 1024, 2048], P(('groups', 'expert'), 'seq'), parts along dimension 0, may hold values from -6 to 6
- key_rows: bfloat16 [4, 1024, 2048], P(('groups', 'expert'), 'seq'), parts along dimension 0, may hold values from -6 to 6
- value_rows: bfloat16 [4, 1024, 2048], P(('groups', 'expert'), 'seq'), parts along dimension 0, may hold values from -6 to 6
- head_gain: float32 [2048], replicated, may hold values from 0.25 to 1.75
- ffn_gain: float32 [2048], replicated, may hold values from 0.25 to 1.75
- expert_ids: int32 [4, 1024, 8], P(('groups', 'expert'), 'seq'), parts along dimension 0, may hold values from 0 to 15, all different within a row; in each aligned block of 128 rows (0 to 127, 128 to 255, ..., all dimensions but the last counted through in order) at most 96 rows name the same one
- router_weight: float32 [4, 1024, 8], P(('groups', 'expert'), 'seq'), parts along dimension 0, may hold values from 0.05 to 1
- w_gate: bfloat16 [16, 2048, 512], P(('seq', 'expert')), may hold values from -0.125 to 0.125
- w_up: bfloat16 [16, 2048, 512], P(('seq', 'expert')), may hold values from -0.125 to 0.125
- w_down: bfloat16 [16, 512, 2048], P(('seq', 'expert')), may hold values from -0.25 to 0.25
Outputs:
- attention: bfloat16 [4, 1024, 2048], P(('groups', 'expert'), 'seq'), parts along dimension 0
- layer_out: bfloat16 [4, 1024, 2048], P(('groups', 'expert'), 'seq'), parts along dimension 0
The draws below stay inside these ranges and needn't reach their ends.
There are 2 independent parts, one for each index of `groups`. The reference program is written for one: setup_inputs(seed, part) draws one part's arguments, and reference() takes and returns one part's arrays. A program takes and returns all parts, laid end to end along the dimension named above; an argument that names none is the same for every part. Nothing has to cross between parts.
Inputs may be any that keep to these rules, and one draw needn't show every extreme that they name: `expert_ids`: each token names 8 different experts. Among the 128 positions k * 128 to (k + 1) * 128 - 1 of one sequence no expert is named more than 96 times, and in every draw some expert is named exactly 96 times there.
All inputs are finite; a program needn't handle non-finite values.
Results may differ from the reference program's by a relative error of at most 0.0075.
Values may be sent and summed in bfloat16 or wider, within the bound.
A program may use at most 128 MiB of HBM per device.

```python
import math
import jax
import jax.numpy as jnp
import numpy as np
from jax import lax

D = 2048
HEADS = 16
HEAD_DIM = 128
TOP = 8
FF = 512
TOK_DEV = 128
EXPERTS = 16
SEQS = 2
LENGTH = 1024
CAP = 96
N_SEQ = 8


def levels(key, shape, pieces, low, largest):
    def one(dim, shards_of):
        heights = jax.random.uniform(jax.random.fold_in(jax.random.fold_in(key, 6), dim), (shards_of,), jnp.float32, low / len(pieces), largest / len(pieces))
        return jnp.repeat(jnp.exp(heights), shape[dim] // shards_of).reshape((-1,) + (1,) * (len(shape) - dim - 1))

    level = one(*pieces[0])
    for cut in pieces[1:]:
        level = level * one(*cut)
    return level


def deal_out(rng, own, number, rows, count, top, bound, lean):
    order = jax.random.permutation(rng, count)
    crowded, ordinary = load_shares(count, rows * top, bound, lean, True), load_shares(count, rows * top, bound, lean, False)
    places = jnp.arange(count)

    def named(sizes, rotation):
        used = int((sizes > 0).sum())
        fixed = max(1, used // 4)
        shifted = fixed + (places - fixed + rotation * (used - fixed)) % max(1, count - fixed)
        return jnp.zeros((count,), jnp.int32).at[order[jnp.where(places < fixed, places, shifted)]].set(jnp.asarray(sizes, jnp.int32))

    sizes = jnp.where(number % 4 == 0, named(crowded, number // 4), named(ordinary, number - number // 4 - 1))
    mixed = jax.random.permutation(jax.random.fold_in(own, 3), count)
    giver, taker = mixed[0:count // 2 * 2:2], mixed[1:count // 2 * 2:2]
    margin = jnp.minimum(sizes[giver] - 1, bound - sizes[taker]) // 2
    margin = jnp.where((giver == order[0]) | (taker == order[0]) | (sizes[taker] == 0), 0, jnp.maximum(margin, 0))
    shifted = jax.random.randint(jax.random.fold_in(own, 4), (count // 2,), 0, 1 << 20) % (margin + 1)
    sizes = sizes.at[giver].add(-shifted).at[taker].add(shifted)
    members = jnp.searchsorted(jnp.cumsum(sizes), jnp.arange(rows * top), side="right").astype(jnp.int32)
    listing = members.reshape(top, rows).T
    listing = listing[jax.random.permutation(jax.random.fold_in(own, 1), rows)]
    rotation = jax.random.randint(jax.random.fold_in(own, 2), (rows, 1), 0, top)
    return jnp.take_along_axis(listing, (jnp.arange(top)[None, :] + rotation) % top, axis=1)


def load_shares(amount, total, most, skew, full):
    portions = [(1 << 20) // math.isqrt(standing ** skew) + 1 for standing in range(1, amount + 1)]
    largest = most if full else min(most, max(-(-total // amount), total * portions[0] // sum(portions)))
    least = 1 if total - largest >= amount - 1 else 0
    given, rest = [largest] + [least] * (amount - 1), total - largest - least * (amount - 1)
    while rest > 0:
        candidates = [i for i in range(1, amount) if given[i] < largest] or [i for i in range(1, amount) if given[i] < most]
        whole, remaining = sum([portions[i] for i in candidates]), rest
        for i in candidates:
            more = min(most - given[i], max(1, remaining * portions[i] // whole), rest)
            given[i] = given[i] + more
            rest = rest - more
    return np.array(given)


def scatter_about(rng, dims, spread, most, pieces=(), held_as=jnp.bfloat16):
    drawn = spread * jax.random.normal(rng, dims, jnp.float32)
    if pieces:
        drawn = drawn * levels(rng, dims, pieces, -0.22, 0.18)
    return jnp.clip(drawn, -most, most).astype(held_as)


def setup_inputs(seed: int = 0, part: int = 0) -> dict:
    splits = jax.random.split(jax.random.key(seed), 11)
    own_keys = jax.random.split(jax.random.fold_in(splits[10], part), 11)
    queries = scatter_about(own_keys[0], (SEQS, LENGTH, D), 1.0, 6.0, ((0, 2), (1, 8)))
    key_rows = scatter_about(own_keys[1], (SEQS, LENGTH, D), 1.0, 6.0, ((0, 2), (1, 8)))
    value_rows = scatter_about(own_keys[2], (SEQS, LENGTH, D), 1.0, 6.0, ((0, 2), (1, 8)))
    head_gain = jnp.clip(1.0 + 0.15 * jax.random.normal(splits[3], (D,), jnp.float32), 0.25, 1.75)
    ffn_gain = jnp.clip(1.0 + 0.15 * jax.random.normal(splits[4], (D,), jnp.float32), 0.25, 1.75)
    expert_ids_keys = jax.random.split(jax.random.fold_in(own_keys[5], 1), SEQS * LENGTH // TOK_DEV)
    expert_ids_turns = jax.random.permutation(jax.random.fold_in(own_keys[5], 3), SEQS * LENGTH // TOK_DEV)
    expert_ids = jax.vmap(lambda own, number: deal_out(jax.random.fold_in(own_keys[5], 2), own, number, TOK_DEV, EXPERTS, TOP, CAP, 2))(expert_ids_keys, expert_ids_turns).reshape((SEQS, LENGTH, TOP))
    router_weight = jnp.clip(jnp.exp(math.log(1.0) - 2.9957323 * jax.random.uniform(own_keys[6], (SEQS, LENGTH, TOP), jnp.float32) ** levels(own_keys[6], (SEQS, LENGTH, TOP), ((0, 2), (1, 8)), -0.2, 0.2)), 0.05, 1.0)
    w_gate = scatter_about(splits[7], (EXPERTS, D, FF), D ** -0.5, 0.125, ((0, 16),))
    w_up = scatter_about(splits[8], (EXPERTS, D, FF), D ** -0.5, 0.125, ((0, 16),))
    w_down = scatter_about(splits[9], (EXPERTS, FF, D), FF ** -0.5, 0.25, ((0, 16),))
    return {"queries": queries, "key_rows": key_rows, "value_rows": value_rows, "head_gain": head_gain, "ffn_gain": ffn_gain, "expert_ids": expert_ids, "router_weight": router_weight, "w_gate": w_gate, "w_up": w_up, "w_down": w_down}


highest = lax.Precision.HIGHEST
epsilon = 1e-06

def mix_heads(sequence):
    query_seq, key_seq, value_seq = sequence
    block_count = LENGTH // 64
    block_shape = (block_count, 64, HEADS, HEAD_DIM)
    query_blocks = query_seq.reshape(block_shape).astype(jnp.float32)
    key_blocks = key_seq.reshape(block_shape).astype(jnp.float32)
    value_blocks = value_seq.reshape(block_shape).astype(jnp.float32)
    causal = jnp.arange(64)[:, None] >= jnp.arange(64)[None, :]

    def advance(state, block):
        query_part, key_part, value_part = block
        scores = jnp.einsum('thd,uhd->htu', query_part, key_part, precision=highest)
        scores = jnp.where(causal, scores, 0.0)
        within = jnp.einsum('htu,uhe->the', scores, value_part, precision=highest)
        before = jnp.einsum('thd,hde->the', query_part, state, precision=highest)
        state = state + jnp.einsum('thd,the->hde', key_part, value_part, precision=highest)
        return (state, within + before)
    start_state = jnp.zeros((HEADS, HEAD_DIM, HEAD_DIM), jnp.float32)
    _, mixed = lax.scan(advance, start_state, (query_blocks, key_blocks, value_blocks))
    return mixed.reshape(LENGTH, HEADS, HEAD_DIM)

def reference(queries, key_rows, value_rows, head_gain, ffn_gain, expert_ids, router_weight, w_gate, w_up, w_down):
    heads_raw = lax.map(mix_heads, (queries, key_rows, value_rows))
    mean_square = lax.optimization_barrier(jnp.mean(heads_raw * heads_raw, axis=-1, keepdims=True))
    attention = ((heads_raw * lax.rsqrt(mean_square + epsilon)).reshape(SEQS, LENGTH, D) * head_gain).astype(jnp.bfloat16)
    attn_float = attention.astype(jnp.float32)
    feature_sq = lax.optimization_barrier(jnp.mean(attn_float * attn_float, axis=-1, keepdims=True))
    normed = (attn_float * lax.rsqrt(feature_sq + epsilon) * ffn_gain).astype(jnp.bfloat16)
    token_total = SEQS * LENGTH
    normed_flat = normed.reshape(token_total, D)
    shares = router_weight / lax.optimization_barrier(jnp.sum(router_weight, axis=-1, keepdims=True))
    share_flat = shares.reshape(token_total * TOP)
    route_flat = expert_ids.reshape(token_total * TOP)
    limit = min(token_total, SEQS * N_SEQ * CAP)

    def add_expert(mixture, packed):
        expert_index, gate_weight, up_weight, down_weight = packed
        position = jnp.nonzero(route_flat == expert_index, size=limit, fill_value=token_total * TOP)[0]
        token_index = position // TOP
        inputs = jnp.take(normed_flat, token_index, axis=0, mode='fill', fill_value=0)
        gate_part = jnp.dot(inputs, gate_weight, preferred_element_type=jnp.float32)
        up_part = jnp.dot(inputs, up_weight, preferred_element_type=jnp.float32)
        expert_hidden = (jax.nn.silu(gate_part) * up_part).astype(jnp.bfloat16)
        expert_out = jnp.dot(expert_hidden, down_weight, preferred_element_type=jnp.float32).astype(jnp.bfloat16)
        weight_rows = jnp.take(share_flat, position, mode='fill', fill_value=0.0)
        mixture = mixture.at[token_index].add(weight_rows[:, None] * expert_out.astype(jnp.float32), mode='drop')
        return (mixture, None)
    mixture_start = jnp.zeros((token_total, D), jnp.float32)
    expert_range = jnp.arange(EXPERTS, dtype=jnp.int32)
    mixture, _ = lax.scan(add_expert, mixture_start, (expert_range, w_gate, w_up, w_down))
    layer_out = (attn_float.reshape(token_total, D) + mixture).astype(jnp.bfloat16).reshape(SEQS, LENGTH, D)
    return (attention, layer_out)
```

```python
import functools

import jax
import jax.numpy as jnp
from jax import lax
from jax.experimental import pallas as pl
from jax.experimental.pallas import tpu as pltpu
from jax.sharding import PartitionSpec as P

HEADS = 16
HEAD_DIM = 128


highest = lax.Precision.HIGHEST
epsilon = 1e-06


def prefix(value, axis, join, neutral):
    count, mine = (lax.axis_size(axis), lax.axis_index(axis))
    pieces = lax.all_gather(value, axis)
    subtotal = jnp.full_like(value, 0) + jnp.asarray(neutral, value.dtype)

    def turn(position, subtotal):
        longer = join(subtotal, pieces[position])
        return jnp.where(position < mine, longer, subtotal)

    return lax.fori_loop(0, count - 1, turn, subtotal)


def add_states(earlier, later):
    return earlier + later


def run_expert(inputs, gate_weight, up_weight, down_weight):
    gate_part = jnp.dot(inputs, gate_weight, preferred_element_type=jnp.float32)
    up_part = jnp.dot(inputs, up_weight, preferred_element_type=jnp.float32)
    expert_hidden = (jax.nn.silu(gate_part) * up_part).astype(jnp.bfloat16)
    return jnp.dot(expert_hidden, down_weight, preferred_element_type=jnp.float32).astype(
        jnp.bfloat16
    )


def to_owners(send_slots):
    return lax.all_to_all(send_slots, ("seq", "expert"), split_axis=0, concat_axis=0, tiled=True)


def from_owners(result_slots):
    return lax.all_to_all(result_slots, ("seq", "expert"), split_axis=0, concat_axis=0, tiled=True)


def per_device_routed(
    queries,
    key_rows,
    value_rows,
    head_gain,
    ffn_gain,
    expert_ids,
    router_weight,
    w_gate,
    w_up,
    w_down,
):
    row_count = queries.shape[1]
    model_width = queries.shape[2]
    block_rows = min(row_count, 512)
    block_count = row_count // block_rows
    block_shape = (block_count, block_rows, HEADS, HEAD_DIM)
    query_blocks = queries.reshape(block_shape)
    key_blocks = key_rows.reshape(block_shape)
    value_blocks = value_rows.reshape(block_shape)
    block_states = jnp.einsum(
        "nthd,nthe->nhde", key_blocks, value_blocks, preferred_element_type=jnp.float32
    )
    local_state = jnp.sum(block_states, axis=0)
    carried = prefix(local_state, "seq", add_states, jnp.zeros_like(local_state))
    starts = carried[None] + jnp.cumsum(block_states, axis=0) - block_states
    causal = jnp.arange(block_rows)[:, None] >= jnp.arange(block_rows)[None, :]
    scores = jnp.einsum(
        "nthd,nuhd->nhtu", query_blocks, key_blocks, preferred_element_type=jnp.float32
    )
    scores = jnp.where(causal, scores, 0.0)
    within = jnp.einsum(
        "nhtu,nuhe->nthe", scores, value_blocks.astype(jnp.float32), precision=highest
    )
    before = jnp.einsum(
        "nthd,nhde->nthe", query_blocks.astype(jnp.float32), starts, precision=highest
    )
    heads_raw = (within + before).reshape(row_count, HEADS, HEAD_DIM)
    mean_square = jnp.mean(heads_raw * heads_raw, axis=-1, keepdims=True)
    attention = (
        (heads_raw * lax.rsqrt(mean_square + epsilon)).reshape(row_count, model_width) * head_gain
    ).astype(jnp.bfloat16)
    attn_float = attention.astype(jnp.float32)
    feature_sq = jnp.mean(attn_float * attn_float, axis=-1, keepdims=True)
    normed = (attn_float * lax.rsqrt(feature_sq + epsilon) * ffn_gain).astype(jnp.bfloat16)
    top_count = expert_ids.shape[2]
    owners = lax.axis_size("seq") * lax.axis_size("expert")
    capacity = min(row_count, 3 * row_count * top_count // (2 * owners))
    slot_total = owners * capacity
    route_flat = expert_ids.reshape(row_count * top_count)
    onehot = (route_flat[:, None] == jnp.arange(owners, dtype=jnp.int32)[None, :]).astype(jnp.int32)
    position = jnp.sum(jnp.cumsum(onehot, axis=0) * onehot, axis=1) - 1
    destination = route_flat * capacity + position
    token_order = jnp.arange(row_count * top_count, dtype=jnp.int32) // top_count
    slot_token = jnp.full((slot_total,), row_count, jnp.int32).at[destination].set(token_order)
    send_slots = jnp.take(normed, slot_token, axis=0, mode="fill", fill_value=0).reshape(
        owners, capacity, model_width
    )
    received = to_owners(send_slots).reshape(slot_total, model_width)
    computed = run_expert(received, w_gate[0], w_up[0], w_down[0])
    returned = from_owners(computed.reshape(owners, capacity, model_width)).reshape(
        slot_total, model_width
    )
    picked = jnp.take(returned, destination, axis=0).reshape(row_count, top_count, model_width)
    shares = router_weight[0] / jnp.sum(router_weight[0], axis=-1, keepdims=True)
    mixture = jnp.einsum("tk,tkd->td", shares, picked.astype(jnp.float32), precision=highest)
    layer_out = (attn_float + mixture).astype(jnp.bfloat16)
    return (
        attention.reshape(1, row_count, model_width),
        layer_out.reshape(1, row_count, model_width),
    )


MESH = pl.DeviceIdType.MESH
VMEM_BYTES = 58 * 1024 * 1024
SCAN_PARTS = 4


def layer_kernel(
    count,
    q_ref, k_ref, v_ref, head_gain, ffn_gain, ids_ref, score_ref, wg_ref, wu_ref, wd_ref,
    att_ref, out_ref,
    w_in, w_out, gates, rows, partial, hidden, share, state, z_pre, z_next, y_pre,
    sum_in, sum_out,
    w_sem, w_send, w_recv, gate_send, gate_recv, z_send, z_recv, y_send, y_recv,
    row_send, row_recv, sum_send, sum_recv,
):
    half_ring = count // 2
    group = lax.axis_index("groups")
    me = lax.axis_index("seq")
    core = lax.axis_index("expert")
    z, y = me // 2, me % 2
    ring = jnp.where(y == 0, z, count - 1 - z)

    def at_ring(place):
        place = lax.rem(place + 2 * count, count)
        seq = jnp.where(place < half_ring, 2 * place, 2 * (count - 1 - place) + 1)
        return (group, seq, core)

    right, left = at_ring(ring + 1), at_ring(ring - 1)
    sibling = (group, me, 1 - core)
    tokens = q_ref.shape[0]
    width = q_ref.shape[1]
    low = tokens // 2
    ff = wg_ref.shape[2]
    part = HEADS // SCAN_PARTS

    barrier = pltpu.get_barrier_semaphore()
    for d in range(1, count):
        pl.semaphore_signal(barrier, inc=1, device_id=at_ring(ring + d), device_id_type=MESH)
    pl.semaphore_signal(barrier, inc=1, device_id=sibling, device_id_type=MESH)

    own_copies = [
        pltpu.make_async_copy(wg_ref.at[0], w_in.at[0], w_sem.at[0]),
        pltpu.make_async_copy(wu_ref.at[0], w_in.at[1], w_sem.at[1]),
        pltpu.make_async_copy(wd_ref.at[0], w_out.at[0], w_sem.at[2]),
    ]
    for c in own_copies:
        c.start()

    def head(h):
        return pl.ds(h * HEAD_DIM, HEAD_DIM)

    for h in range(HEADS):
        state[head(h), :] = lax.dot_general(
            k_ref[:, head(h)], v_ref[:, head(h)], (((0,), (0,)), ((), ())),
            preferred_element_type=jnp.float32,
        )

    lanes = lax.broadcasted_iota(jnp.int32, (tokens, 128), 1)
    scores = score_ref[...]
    named = scores / jnp.sum(scores, axis=-1, keepdims=True)
    ids = ids_ref[...]
    dense = jnp.zeros((tokens, 128), jnp.float32)
    for t in range(ids.shape[1]):
        dense += jnp.where(ids[:, t : t + 1] == lanes, named[:, t : t + 1], 0.0)
    experts = gates.shape[2]
    gates[0, 0] = jnp.transpose(dense)[:experts, :]

    pl.semaphore_wait(barrier, count)

    def remote(src, dst, send, recv, where):
        return pltpu.make_async_remote_copy(
            src_ref=src, dst_ref=dst, send_sem=send, recv_sem=recv,
            device_id=where, device_id_type=MESH,
        )

    def span(j):
        return pl.ds(j * part * HEAD_DIM, part * HEAD_DIM)

    def z_copy(j):
        up = (group, lax.rem(me + 2, count), core)
        return remote(z_next.at[span(j)], z_pre.at[span(j)], z_send.at[j], z_recv.at[j], up)

    across = (group, me + 1 - 2 * y, core)

    def y_copy(j, src):
        return remote(src.at[span(j)], y_pre.at[span(j)], y_send.at[j], y_recv.at[j], across)

    for j in range(SCAN_PARTS):
        @pl.when(z == 0)
        def _():
            z_pre[span(j), :] = jnp.zeros((part * HEAD_DIM, HEAD_DIM), jnp.bfloat16)

        @pl.when(z > 0)
        def _():
            z_copy(j).wait_recv()

        z_next[span(j), :] = (
            z_pre[span(j), :].astype(jnp.float32) + state[span(j), :]
        ).astype(jnp.bfloat16)

        @pl.when(z < half_ring - 1)
        def _():
            z_copy(j).start()

        @pl.when(y == 0)
        def _():
            y_copy(j, z_next).start()

        @pl.when(y == 1)
        def _():
            y_copy(j, z_pre).start()

    gate_copies = []
    for d in range(1, count):
        slot = (d, 0) if d < half_ring else ((0, 1) if d == half_ring else (count - d, 1))
        gate_copies.append(
            remote(gates.at[0, 0], gates.at[slot[0], slot[1]],
                   gate_send.at[slot[0], slot[1]], gate_recv.at[slot[0], slot[1]],
                   at_ring(ring + d))
        )
    for c in gate_copies:
        c.start()
    weight_copies = [
        remote(wg_ref.at[0], w_in.at[2], w_send.at[0], w_recv.at[0], sibling),
        remote(wu_ref.at[0], w_in.at[3], w_send.at[1], w_recv.at[1], sibling),
        remote(wd_ref.at[0], w_out.at[1], w_send.at[2], w_recv.at[2], sibling),
    ]
    for c in weight_copies:
        c.start()

    causal = lax.broadcasted_iota(jnp.int32, (tokens, tokens), 0) >= lax.broadcasted_iota(
        jnp.int32, (tokens, tokens), 1
    )
    square = jnp.zeros((tokens, HEAD_DIM), jnp.float32)
    for j in range(SCAN_PARTS):
        y_copy(j, z_next).wait_recv()
        for h in range(j * part, (j + 1) * part):
            q, k, v = q_ref[:, head(h)], k_ref[:, head(h)], v_ref[:, head(h)]
            start = (
                z_pre[head(h), :].astype(jnp.float32) + y_pre[head(h), :].astype(jnp.float32)
            ).astype(jnp.bfloat16)
            pair = lax.dot_general(
                q, k, (((1,), (1,)), ((), ())), preferred_element_type=jnp.float32
            )
            pair = jnp.where(causal, pair, 0.0).astype(jnp.bfloat16)
            raw = jnp.dot(pair, v, preferred_element_type=jnp.float32) + jnp.dot(
                q, start, preferred_element_type=jnp.float32
            )
            mean_square = jnp.mean(raw * raw, axis=-1, keepdims=True)
            att = (raw * lax.rsqrt(mean_square + epsilon) * head_gain[:, head(h)]).astype(
                jnp.bfloat16
            )
            att_ref[:, head(h)] = att
            att = att.astype(jnp.float32)
            square += att * att
    scale = lax.rsqrt(jnp.sum(square, axis=-1, keepdims=True) / width + epsilon)
    for h in range(HEADS):
        rows[0, pl.ds(0, tokens), head(h)] = (
            att_ref[:, head(h)].astype(jnp.float32) * scale * ffn_gain[:, head(h)]
        ).astype(jnp.bfloat16)

    def row_span(side, h):
        return pl.ds(side * tokens + h * low, low)

    def row_copy(side, step, h):
        src = rows.at[step - 1, row_span(0 if step == 1 else side, h)]
        if step < half_ring:
            dst = rows.at[step, row_span(side, h)]
        else:
            dst = rows.at[0, row_span(1, h)]
        return remote(
            src, dst, row_send.at[side, step - 1, h], row_recv.at[side, step - 1, h],
            right if side == 0 else left,
        )

    for h in range(2):
        for side in range(2):
            row_copy(side, 1, h).start()

    for c in own_copies:
        c.wait()
    for c in weight_copies:
        c.wait_recv()
    for c in gate_copies:
        c.wait_recv()

    def run_experts(index):
        picks = lax.broadcasted_iota(jnp.int32, (experts, 128), 0)
        for e, owner in ((0, 2 * me + core), (1, 2 * me + 1 - core)):
            chosen = (picks == owner).astype(jnp.float32)
            for side in range(2):
                share[e, pl.ds(side * tokens, tokens), :] = lax.dot_general(
                    gates[index, side], chosen, (((0,), (0,)), ((), ())),
                    preferred_element_type=jnp.float32, precision=highest,
                )
        tile = 256
        for e in range(2):
            @pl.loop(0, ff // tile)
            def _(n):
                cols = pl.ds(pl.multiple_of(n * tile, tile), tile)
                x = rows[index]
                gate_part = jnp.dot(
                    x, w_in[2 * e, :, cols], preferred_element_type=jnp.float32
                )
                up_part = jnp.dot(
                    x, w_in[2 * e + 1, :, cols], preferred_element_type=jnp.float32
                )
                act = gate_part / (1.0 + jnp.exp(-gate_part)) * up_part
                hidden[:, pl.ds(pl.multiple_of(e * ff + n * tile, tile), tile)] = (
                    act * share[e, :, 0:1]
                ).astype(jnp.bfloat16)

        @pl.loop(0, width // tile)
        def _(n):
            cols = pl.ds(pl.multiple_of(n * tile, tile), tile)
            partial[index, :, cols] = jnp.dot(
                hidden[:, pl.ds(0, ff)], w_out[0, :, cols], preferred_element_type=jnp.float32
            ) + jnp.dot(
                hidden[:, pl.ds(ff, ff)], w_out[1, :, cols], preferred_element_type=jnp.float32
            )

    def sum_copy(side, step, h):
        here = (side, step - 1, pl.ds(h * low, low))
        return remote(
            sum_out.at[here], sum_in.at[here],
            sum_send.at[side, step - 1, h], sum_recv.at[side, step - 1, h],
            right if side == 0 else left,
        )

    def sum_step(side, step, h):
        index = half_ring - step + 1 if step > 1 else 0
        value = partial[index, row_span(1 if step == 1 else 1 - side, h), :]
        if step > 2 or (step == 2 and h == side):
            sum_copy(side, step - 1, h).wait_recv()
            value += sum_in[side, step - 2, pl.ds(h * low, low), :].astype(jnp.float32)
        sum_out[side, step - 1, pl.ds(h * low, low), :] = value.astype(jnp.bfloat16)
        sum_copy(side, step, h).start()

    for step in range(1, half_ring):
        for h in range(2):
            for side in range(2):
                row_copy(side, step, h).wait_recv()
                if step + 1 < half_ring or h == side:
                    row_copy(side, step + 1, h).start()
        run_experts(step)
    for side in range(2):
        sum_step(side, 2, 1 - side)
    for side in range(2):
        row_copy(side, half_ring, side).wait_recv()
    run_experts(0)
    for side in range(2):
        sum_step(side, 1, side)
    for side in range(2):
        sum_step(side, 2, side)
    for step in range(3, half_ring + 1):
        for first in range(2):
            for side in range(2):
                sum_step(side, step, (1 - side + first) % 2)
    for h in range(2):
        total = partial[0, row_span(0, h), :] + att_ref[pl.ds(h * low, low), :].astype(jnp.float32)
        for side in range(2):
            sum_copy(side, half_ring, h).wait_recv()
            total += sum_in[side, half_ring - 1, pl.ds(h * low, low), :].astype(jnp.float32)
        out_ref[pl.ds(h * low, low), :] = total.astype(jnp.bfloat16)

    for c in weight_copies + gate_copies:
        c.wait_send()
    for j in range(SCAN_PARTS):
        @pl.when(z < half_ring - 1)
        def _():
            z_copy(j).wait_send()

        y_copy(j, z_next).wait_send()
    for side in range(2):
        for step in range(1, half_ring + 1):
            for h in range(2):
                if step < half_ring or h == side:
                    row_copy(side, step, h).wait_send()
                if step > 1 or h == side:
                    sum_copy(side, step, h).wait_send()


def per_device_ring(
    experts,
    queries,
    key_rows,
    value_rows,
    head_gain,
    ffn_gain,
    expert_ids,
    router_weight,
    w_gate,
    w_up,
    w_down,
):
    count = lax.axis_size("seq")
    half_ring = count // 2
    tokens, width = queries.shape[1:]
    ff = w_gate.shape[2]
    bf16, f32 = jnp.bfloat16, jnp.float32
    vmem = pl.BlockSpec(memory_space=pltpu.VMEM)
    hbm = pl.BlockSpec(memory_space=pl.ANY)
    dma = pltpu.SemaphoreType.DMA
    states = (HEADS * HEAD_DIM, HEAD_DIM)
    attention, layer_out = pl.pallas_call(
        functools.partial(layer_kernel, count),
        out_shape=[jax.ShapeDtypeStruct((tokens, width), bf16)] * 2,
        in_specs=[vmem] * 7 + [hbm] * 3,
        out_specs=[vmem] * 2,
        scratch_shapes=[
            pltpu.VMEM((4, width, ff), bf16),
            pltpu.VMEM((2, ff, width), bf16),
            pltpu.VMEM((half_ring, 2, experts, tokens), f32),
            pltpu.VMEM((half_ring, 2 * tokens, width), bf16),
            pltpu.VMEM((half_ring, 2 * tokens, width), f32),
            pltpu.VMEM((2 * tokens, 2 * ff), bf16),
            pltpu.VMEM((2, 2 * tokens, 128), f32),
            pltpu.VMEM(states, f32),
            pltpu.VMEM(states, bf16),
            pltpu.VMEM(states, bf16),
            pltpu.VMEM(states, bf16),
            pltpu.VMEM((2, half_ring, tokens, width), bf16),
            pltpu.VMEM((2, half_ring, tokens, width), bf16),
            dma((3,)),
            dma((3,)),
            dma((3,)),
            dma((half_ring, 2)),
            dma((half_ring, 2)),
            dma((SCAN_PARTS,)),
            dma((SCAN_PARTS,)),
            dma((SCAN_PARTS,)),
            dma((SCAN_PARTS,)),
            dma((2, half_ring, 2)),
            dma((2, half_ring, 2)),
            dma((2, half_ring, 2)),
            dma((2, half_ring, 2)),
        ],
        compiler_params=pltpu.CompilerParams(
            collective_id=0, has_side_effects=True, vmem_limit_bytes=VMEM_BYTES
        ),
        cost_estimate=pl.CostEstimate(
            flops=12 * count * tokens * width * ff,
            bytes_accessed=6 * width * ff + 10 * tokens * width,
            transcendentals=2 * count * tokens * ff,
        ),
    )(
        queries[0],
        key_rows[0],
        value_rows[0],
        head_gain.reshape(1, width),
        ffn_gain.reshape(1, width),
        expert_ids[0],
        router_weight[0],
        w_gate,
        w_up,
        w_down,
    )
    return attention[None], layer_out[None]


def fits_in_vmem(mesh, arrays):
    count = mesh.shape["seq"]
    queries, w_gate = arrays[0], arrays[7]
    tokens, width = queries.shape[1] // count, queries.shape[2]
    held = count * tokens * width * (2 + 4 + 2 + 2) + 12 * width * w_gate.shape[2]
    return held < VMEM_BYTES * 3 // 4


def solution(mesh):
    def layer(*arrays):
        if fits_in_vmem(mesh, arrays):
            body = functools.partial(per_device_ring, arrays[7].shape[0])
        else:
            body = per_device_routed
        return mapped(body)(*arrays)

    def mapped(body):
        return jax.shard_map(
            body,
            mesh=mesh,
            in_specs=(
                P(("groups", "expert"), "seq", None),
                P(("groups", "expert"), "seq", None),
                P(("groups", "expert"), "seq", None),
                P(),
                P(),
                P(("groups", "expert"), "seq", None),
                P(("groups", "expert"), "seq", None),
                P(("seq", "expert"), None, None),
                P(("seq", "expert"), None, None),
                P(("seq", "expert"), None, None),
            ),
            out_specs=(P(("groups", "expert"), "seq", None), P(("groups", "expert"), "seq", None)),
            check_vma=False,
        )

    return layer
```

```python
import functools

import jax
import jax.numpy as jnp
from jax import lax
from jax.experimental import pallas as pl
from jax.experimental.pallas import tpu as pltpu
from jax.sharding import PartitionSpec as P

HEADS = 16
HEAD_DIM = 128


highest = lax.Precision.HIGHEST
epsilon = 1e-06


def prefix(value, axis, join, neutral):
    count, mine = (lax.axis_size(axis), lax.axis_index(axis))
    pieces = lax.all_gather(value, axis)
    subtotal = jnp.full_like(value, 0) + jnp.asarray(neutral, value.dtype)

    def turn(position, subtotal):
        longer = join(subtotal, pieces[position])
        return jnp.where(position < mine, longer, subtotal)

    return lax.fori_loop(0, count - 1, turn, subtotal)


def add_states(earlier, later):
    return earlier + later


def run_expert(inputs, gate_weight, up_weight, down_weight):
    gate_part = jnp.dot(inputs, gate_weight, preferred_element_type=jnp.float32)
    up_part = jnp.dot(inputs, up_weight, preferred_element_type=jnp.float32)
    expert_hidden = (jax.nn.silu(gate_part) * up_part).astype(jnp.bfloat16)
    return jnp.dot(expert_hidden, down_weight, preferred_element_type=jnp.float32).astype(
        jnp.bfloat16
    )


def to_owners(send_slots):
    return lax.all_to_all(send_slots, ("seq", "expert"), split_axis=0, concat_axis=0, tiled=True)


def from_owners(result_slots):
    return lax.all_to_all(result_slots, ("seq", "expert"), split_axis=0, concat_axis=0, tiled=True)


def per_device_routed(
    queries,
    key_rows,
    value_rows,
    head_gain,
    ffn_gain,
    expert_ids,
    router_weight,
    w_gate,
    w_up,
    w_down,
):
    row_count = queries.shape[1]
    model_width = queries.shape[2]
    block_rows = min(row_count, 512)
    block_count = row_count // block_rows
    block_shape = (block_count, block_rows, HEADS, HEAD_DIM)
    query_blocks = queries.reshape(block_shape)
    key_blocks = key_rows.reshape(block_shape)
    value_blocks = value_rows.reshape(block_shape)
    block_states = jnp.einsum(
        "nthd,nthe->nhde", key_blocks, value_blocks, preferred_element_type=jnp.float32
    )
    local_state = jnp.sum(block_states, axis=0)
    carried = prefix(local_state, "seq", add_states, jnp.zeros_like(local_state))
    starts = carried[None] + jnp.cumsum(block_states, axis=0) - block_states
    causal = jnp.arange(block_rows)[:, None] >= jnp.arange(block_rows)[None, :]
    scores = jnp.einsum(
        "nthd,nuhd->nhtu", query_blocks, key_blocks, preferred_element_type=jnp.float32
    )
    scores = jnp.where(causal, scores, 0.0)
    within = jnp.einsum(
        "nhtu,nuhe->nthe", scores, value_blocks.astype(jnp.float32), precision=highest
    )
    before = jnp.einsum(
        "nthd,nhde->nthe", query_blocks.astype(jnp.float32), starts, precision=highest
    )
    heads_raw = (within + before).reshape(row_count, HEADS, HEAD_DIM)
    mean_square = jnp.mean(heads_raw * heads_raw, axis=-1, keepdims=True)
    attention = (
        (heads_raw * lax.rsqrt(mean_square + epsilon)).reshape(row_count, model_width) * head_gain
    ).astype(jnp.bfloat16)
    attn_float = attention.astype(jnp.float32)
    feature_sq = jnp.mean(attn_float * attn_float, axis=-1, keepdims=True)
    normed = (attn_float * lax.rsqrt(feature_sq + epsilon) * ffn_gain).astype(jnp.bfloat16)
    top_count = expert_ids.shape[2]
    owners = lax.axis_size("seq") * lax.axis_size("expert")
    capacity = min(row_count, 3 * row_count * top_count // (2 * owners))
    slot_total = owners * capacity
    route_flat = expert_ids.reshape(row_count * top_count)
    onehot = (route_flat[:, None] == jnp.arange(owners, dtype=jnp.int32)[None, :]).astype(jnp.int32)
    position = jnp.sum(jnp.cumsum(onehot, axis=0) * onehot, axis=1) - 1
    destination = route_flat * capacity + position
    token_order = jnp.arange(row_count * top_count, dtype=jnp.int32) // top_count
    slot_token = jnp.full((slot_total,), row_count, jnp.int32).at[destination].set(token_order)
    send_slots = jnp.take(normed, slot_token, axis=0, mode="fill", fill_value=0).reshape(
        owners, capacity, model_width
    )
    received = to_owners(send_slots).reshape(slot_total, model_width)
    computed = run_expert(received, w_gate[0], w_up[0], w_down[0])
    returned = from_owners(computed.reshape(owners, capacity, model_width)).reshape(
        slot_total, model_width
    )
    picked = jnp.take(returned, destination, axis=0).reshape(row_count, top_count, model_width)
    shares = router_weight[0] / jnp.sum(router_weight[0], axis=-1, keepdims=True)
    mixture = jnp.einsum("tk,tkd->td", shares, picked.astype(jnp.float32), precision=highest)
    layer_out = (attn_float + mixture).astype(jnp.bfloat16)
    return (
        attention.reshape(1, row_count, model_width),
        layer_out.reshape(1, row_count, model_width),
    )


MESH = pl.DeviceIdType.MESH
VMEM_BYTES = 58 * 1024 * 1024
SCAN_PARTS = 4
ROW_PARTS = 4


def layer_kernel(
    count,
    q_ref, k_ref, v_ref, head_gain, ffn_gain, ids_ref, score_ref, wg_ref, wu_ref, wd_ref,
    att_ref, out_ref,
    w_in, w_out, gates, rows, normed, partial, hidden, share, state, within,
    a_out, a_in, c_out, c_in, b_out, b_in, sum_in, sum_out,
    w_sem, w_send, w_recv, gate_send, gate_recv, a_send, a_recv, c_send, c_recv, b_send, b_recv,
    row_send, row_recv, sum_send, sum_recv,
):
    half_ring = count // 2
    group = lax.axis_index("groups")
    me = lax.axis_index("seq")
    core = lax.axis_index("expert")
    z, y = me // 2, me % 2
    ring = jnp.where(y == 0, z, count - 1 - z)

    def at_ring(place):
        place = lax.rem(place + 2 * count, count)
        seq = jnp.where(place < half_ring, 2 * place, 2 * (count - 1 - place) + 1)
        return (group, seq, core)

    right, left = at_ring(ring + 1), at_ring(ring - 1)
    sibling = (group, me, 1 - core)
    tokens = q_ref.shape[0]
    width = q_ref.shape[1]
    low = tokens // 2
    ff = wg_ref.shape[2]
    part = HEADS // SCAN_PARTS

    barrier = pltpu.get_barrier_semaphore()
    for d in range(1, count):
        pl.semaphore_signal(barrier, inc=1, device_id=at_ring(ring + d), device_id_type=MESH)
    pl.semaphore_signal(barrier, inc=1, device_id=sibling, device_id_type=MESH)

    own_copies = [
        pltpu.make_async_copy(wg_ref.at[0], w_in.at[0], w_sem.at[0]),
        pltpu.make_async_copy(wu_ref.at[0], w_in.at[1], w_sem.at[1]),
        pltpu.make_async_copy(wd_ref.at[0], w_out.at[0], w_sem.at[2]),
    ]
    for c in own_copies:
        c.start()

    def head(h):
        return pl.ds(h * HEAD_DIM, HEAD_DIM)

    for h in range(HEADS):
        state[head(h), :] = lax.dot_general(
            k_ref[:, head(h)], v_ref[:, head(h)], (((0,), (0,)), ((), ())),
            preferred_element_type=jnp.float32,
        )

    gate_rows = gates.shape[2] - 8
    picks = lax.broadcasted_iota(jnp.int32, (gate_rows, tokens), 0)
    scores = score_ref[...]
    named = scores / jnp.sum(scores, axis=0, keepdims=True)
    ids = ids_ref[...]
    dense = jnp.zeros((gate_rows, tokens), jnp.float32)
    for t in range(ids.shape[0]):
        dense += jnp.where(ids[t : t + 1, :] == picks, named[t : t + 1, :], 0.0)
    gates[0, 0, pl.ds(0, gate_rows), :] = dense

    pl.semaphore_wait(barrier, count)

    def remote(src, dst, send, recv, where):
        return pltpu.make_async_remote_copy(
            src_ref=src, dst_ref=dst, send_sem=send, recv_sem=recv,
            device_id=where, device_id_type=MESH,
        )

    half_rows = HEADS * HEAD_DIM // 2
    piece = half_rows // SCAN_PARTS
    mine, other = y * half_rows, (1 - y) * half_rows
    across = (group, me + 1 - 2 * y, core)
    above = (group, lax.rem(me + 2, count), core)

    def span(j, base=0):
        return pl.ds(pl.multiple_of(base + j * piece, piece), piece)

    def a_copy(j):
        return remote(a_out.at[span(j)], a_in.at[span(j)], a_send.at[j], a_recv.at[j], across)

    def b_copy(j):
        return remote(b_out.at[span(j)], b_in.at[span(j)], b_send.at[j], b_recv.at[j], across)

    def c_copy(j):
        return remote(c_out.at[span(j)], c_in.at[span(j)], c_send.at[j], c_recv.at[j], above)

    for j in range(SCAN_PARTS):
        a_out[span(j), :] = state[span(j, other), :].astype(jnp.bfloat16)
        a_copy(j).start()
    weight_copies = [
        remote(wg_ref.at[0], w_in.at[2], w_send.at[0], w_recv.at[0], sibling),
        remote(wu_ref.at[0], w_in.at[3], w_send.at[1], w_recv.at[1], sibling),
        remote(wd_ref.at[0], w_out.at[1], w_send.at[2], w_recv.at[2], sibling),
    ]
    for c in weight_copies:
        c.start()

    causal = lax.broadcasted_iota(jnp.int32, (tokens, tokens), 0) >= lax.broadcasted_iota(
        jnp.int32, (tokens, tokens), 1
    )
    for h in range(HEADS):
        pair = lax.dot_general(
            q_ref[:, head(h)], k_ref[:, head(h)], (((1,), (1,)), ((), ())),
            preferred_element_type=jnp.float32,
        )
        pair = jnp.where(causal, pair, 0.0).astype(jnp.bfloat16)
        within[:, head(h)] = jnp.dot(pair, v_ref[:, head(h)], preferred_element_type=jnp.float32)

    for j in range(SCAN_PARTS):
        a_copy(j).wait_recv()

        @pl.when(z == 0)
        def _():
            c_in[span(j), :] = jnp.zeros((piece, HEAD_DIM), jnp.bfloat16)

        @pl.when(z > 0)
        def _():
            c_copy(j).wait_recv()

        earlier = c_in[span(j), :].astype(jnp.float32)
        own = state[span(j, mine), :]
        c_out[span(j), :] = (
            earlier + (own + a_in[span(j), :].astype(jnp.float32))
        ).astype(jnp.bfloat16)

        @pl.when(z < half_ring - 1)
        def _():
            c_copy(j).start()

        b_out[span(j), :] = (earlier + jnp.where(y == 0, own, 0.0)).astype(jnp.bfloat16)
        b_copy(j).start()

    part_width = width // ROW_PARTS

    def row_copy(side, step, i, origin):
        place = lax.rem(origin + 2 * count, count)
        first = jnp.where(place < half_ring, 0, ROW_PARTS // 2)
        c = lax.rem(first + i, ROW_PARTS)
        cols = pl.ds(pl.multiple_of(c * part_width, part_width), part_width)
        src = rows.at[step - 1, pl.ds(0 if step == 1 else side * tokens, tokens), cols]
        if step < half_ring:
            dst = rows.at[step, pl.ds(side * tokens, tokens), cols]
        else:
            dst = rows.at[0, pl.ds(tokens, tokens), cols]
        return remote(
            src, dst, row_send.at[side, step - 1, i], row_recv.at[side, step - 1, i],
            right if side == 0 else left,
        )

    def row_out(side, step, i):
        back = step - 1
        return row_copy(side, step, i, ring - back if side == 0 else ring + back)

    def row_arrival(side, step, i):
        return row_copy(side, step, i, ring - step if side == 0 else ring + step)

    def goes(side, step, i):
        return step < half_ring or (i < ROW_PARTS // 2) == (side == 0)

    square = jnp.zeros((tokens, HEAD_DIM), jnp.float32)
    heads_each = piece // HEAD_DIM
    for j in range(2 * SCAN_PARTS):
        if j < SCAN_PARTS:
            base, k = mine, j
            start = c_in[span(k), :].astype(jnp.float32) + jnp.where(
                y == 1, a_in[span(k), :].astype(jnp.float32), 0.0
            )
            start = start.astype(jnp.bfloat16)
        else:
            base, k = other, j - SCAN_PARTS
            b_copy(k).wait_recv()
            start = b_in[span(k), :]
        for i in range(heads_each):
            cols = pl.ds(
                pl.multiple_of(base + k * piece + i * HEAD_DIM, HEAD_DIM), HEAD_DIM
            )
            raw = within[:, cols] + jnp.dot(
                q_ref[:, cols], start[i * HEAD_DIM : (i + 1) * HEAD_DIM],
                preferred_element_type=jnp.float32,
            )
            mean_square = jnp.mean(raw * raw, axis=-1, keepdims=True)
            att = (raw * lax.rsqrt(mean_square + epsilon) * head_gain[:, cols]).astype(
                jnp.bfloat16
            )
            att_ref[:, cols] = att
            rows[0, pl.ds(0, tokens), cols] = att
            att = att.astype(jnp.float32)
            square += att * att
        if (j + 1) % (2 * SCAN_PARTS // ROW_PARTS) == 0:
            for side in range(2):
                row_out(side, 1, j // (2 * SCAN_PARTS // ROW_PARTS)).start()

    scale = lax.rsqrt(jnp.sum(jnp.transpose(square), axis=0, keepdims=True) / width + epsilon)
    gates[0, 0, pl.ds(gate_rows, 8), :] = jnp.broadcast_to(scale, (8, tokens))
    gate_copies = []
    for d in range(1, count):
        slot = (d, 0) if d < half_ring else ((0, 1) if d == half_ring else (count - d, 1))
        gate_copies.append(
            remote(gates.at[0, 0], gates.at[slot[0], slot[1]],
                   gate_send.at[slot[0], slot[1]], gate_recv.at[slot[0], slot[1]],
                   at_ring(ring + d))
        )
    for c in gate_copies:
        c.start()

    def row_span(side, h):
        return pl.ds(side * tokens + h * low, low)

    for c in own_copies:
        c.wait()
    for c in weight_copies:
        c.wait_recv()
    for c in gate_copies:
        c.wait_recv()

    def run_experts(index):
        line = lax.broadcasted_iota(jnp.int32, (gate_rows + 8, 128), 0)
        for e, owner in enumerate((2 * me + core, 2 * me + 1 - core, gate_rows)):
            chosen = (line == owner).astype(jnp.float32)
            for side in range(2):
                share[e, pl.ds(side * tokens, tokens), :] = lax.dot_general(
                    gates[index, side], chosen, (((0,), (0,)), ((), ())),
                    preferred_element_type=jnp.float32, precision=highest,
                )
        tile = 256

        @pl.loop(0, width // tile)
        def _(n):
            cols = pl.ds(pl.multiple_of(n * tile, tile), tile)
            normed[:, cols] = (
                rows[index, :, cols].astype(jnp.float32) * share[2, :, 0:1] * ffn_gain[:, cols]
            ).astype(jnp.bfloat16)

        for e in range(2):
            @pl.loop(0, ff // tile)
            def _(n):
                cols = pl.ds(pl.multiple_of(n * tile, tile), tile)
                x = normed[...]
                gate_part = jnp.dot(
                    x, w_in[2 * e, :, cols], preferred_element_type=jnp.float32
                )
                up_part = jnp.dot(
                    x, w_in[2 * e + 1, :, cols], preferred_element_type=jnp.float32
                )
                act = gate_part / (1.0 + jnp.exp(-gate_part)) * up_part
                hidden[:, pl.ds(pl.multiple_of(e * ff + n * tile, tile), tile)] = (
                    act * share[e, :, 0:1]
                ).astype(jnp.bfloat16)

        @pl.loop(0, width // tile)
        def _(n):
            cols = pl.ds(pl.multiple_of(n * tile, tile), tile)
            partial[index, :, cols] = jnp.dot(
                hidden[:, pl.ds(0, ff)], w_out[0, :, cols], preferred_element_type=jnp.float32
            ) + jnp.dot(
                hidden[:, pl.ds(ff, ff)], w_out[1, :, cols], preferred_element_type=jnp.float32
            )

    def sum_copy(side, step, h):
        here = (side, step - 1, pl.ds(h * low, low))
        return remote(
            sum_out.at[here], sum_in.at[here],
            sum_send.at[side, step - 1, h], sum_recv.at[side, step - 1, h],
            right if side == 0 else left,
        )

    def sum_step(side, step, h):
        index = half_ring - step + 1 if step > 1 else 0
        value = partial[index, row_span(1 if step == 1 else 1 - side, h), :]
        if step > 2 or (step == 2 and h == side):
            sum_copy(side, step - 1, h).wait_recv()
            value += sum_in[side, step - 2, pl.ds(h * low, low), :].astype(jnp.float32)
        sum_out[side, step - 1, pl.ds(h * low, low), :] = value.astype(jnp.bfloat16)
        sum_copy(side, step, h).start()

    for step in range(1, half_ring):
        for i in range(ROW_PARTS):
            for side in range(2):
                row_arrival(side, step, i).wait_recv()
                if goes(side, step + 1, i):
                    row_out(side, step + 1, i).start()
        run_experts(step)
    for side in range(2):
        sum_step(side, 2, 1 - side)
    for i in range(ROW_PARTS):
        for side in range(2):
            if goes(side, half_ring, i):
                row_arrival(side, half_ring, i).wait_recv()
    run_experts(0)
    for side in range(2):
        sum_step(side, 1, side)
    for side in range(2):
        sum_step(side, 2, side)
    for step in range(3, half_ring + 1):
        for first in range(2):
            for side in range(2):
                sum_step(side, step, (1 - side + first) % 2)
    for h in range(2):
        total = partial[0, row_span(0, h), :] + att_ref[pl.ds(h * low, low), :].astype(jnp.float32)
        for side in range(2):
            sum_copy(side, half_ring, h).wait_recv()
            total += sum_in[side, half_ring - 1, pl.ds(h * low, low), :].astype(jnp.float32)
        out_ref[pl.ds(h * low, low), :] = total.astype(jnp.bfloat16)

    for c in weight_copies + gate_copies:
        c.wait_send()
    for j in range(SCAN_PARTS):
        @pl.when(z < half_ring - 1)
        def _():
            c_copy(j).wait_send()

        a_copy(j).wait_send()
        b_copy(j).wait_send()
    for side in range(2):
        for step in range(1, half_ring + 1):
            for i in range(ROW_PARTS):
                if goes(side, step, i):
                    row_out(side, step, i).wait_send()
            for h in range(2):
                if step > 1 or h == side:
                    sum_copy(side, step, h).wait_send()


def per_device_ring(
    experts,
    queries,
    key_rows,
    value_rows,
    head_gain,
    ffn_gain,
    expert_ids,
    router_weight,
    w_gate,
    w_up,
    w_down,
):
    count = lax.axis_size("seq")
    half_ring = count // 2
    tokens, width = queries.shape[1:]
    ff = w_gate.shape[2]
    bf16, f32 = jnp.bfloat16, jnp.float32
    vmem = pl.BlockSpec(memory_space=pltpu.VMEM)
    hbm = pl.BlockSpec(memory_space=pl.ANY)
    dma = pltpu.SemaphoreType.DMA
    states = (HEADS * HEAD_DIM, HEAD_DIM)
    half_states = (HEADS * HEAD_DIM // 2, HEAD_DIM)
    gate_rows = -(-experts // 8) * 8 + 8
    attention, layer_out = pl.pallas_call(
        functools.partial(layer_kernel, count),
        out_shape=[jax.ShapeDtypeStruct((tokens, width), bf16)] * 2,
        in_specs=[vmem] * 7 + [hbm] * 3,
        out_specs=[vmem] * 2,
        scratch_shapes=[
            pltpu.VMEM((4, width, ff), bf16),
            pltpu.VMEM((2, ff, width), bf16),
            pltpu.VMEM((half_ring, 2, gate_rows, tokens), f32),
            pltpu.VMEM((half_ring, 2 * tokens, width), bf16),
            pltpu.VMEM((2 * tokens, width), bf16),
            pltpu.VMEM((half_ring, 2 * tokens, width), f32),
            pltpu.VMEM((2 * tokens, 2 * ff), bf16),
            pltpu.VMEM((3, 2 * tokens, 128), f32),
            pltpu.VMEM(states, f32),
            pltpu.VMEM((tokens, width), f32),
            pltpu.VMEM(half_states, bf16),
            pltpu.VMEM(half_states, bf16),
            pltpu.VMEM(half_states, bf16),
            pltpu.VMEM(half_states, bf16),
            pltpu.VMEM(half_states, bf16),
            pltpu.VMEM(half_states, bf16),
            pltpu.VMEM((2, half_ring, tokens, width), bf16),
            pltpu.VMEM((2, half_ring, tokens, width), bf16),
            dma((3,)),
            dma((3,)),
            dma((3,)),
            dma((half_ring, 2)),
            dma((half_ring, 2)),
            dma((SCAN_PARTS,)),
            dma((SCAN_PARTS,)),
            dma((SCAN_PARTS,)),
            dma((SCAN_PARTS,)),
            dma((SCAN_PARTS,)),
            dma((SCAN_PARTS,)),
            dma((2, half_ring, ROW_PARTS)),
            dma((2, half_ring, ROW_PARTS)),
            dma((2, half_ring, 2)),
            dma((2, half_ring, 2)),
        ],
        compiler_params=pltpu.CompilerParams(
            collective_id=0, has_side_effects=True, vmem_limit_bytes=VMEM_BYTES
        ),
        cost_estimate=pl.CostEstimate(
            flops=12 * count * tokens * width * ff,
            bytes_accessed=6 * width * ff + 10 * tokens * width,
            transcendentals=2 * count * tokens * ff,
        ),
    )(
        queries[0],
        key_rows[0],
        value_rows[0],
        head_gain.reshape(1, width),
        ffn_gain.reshape(1, width),
        expert_ids[0].T,
        router_weight[0].T,
        w_gate,
        w_up,
        w_down,
    )
    return attention[None], layer_out[None]


def fits_in_vmem(mesh, arrays):
    count = mesh.shape["seq"]
    queries, w_gate = arrays[0], arrays[7]
    tokens, width = queries.shape[1] // count, queries.shape[2]
    held = count * tokens * width * (2 + 4 + 2 + 2) + 12 * width * w_gate.shape[2]
    return held < VMEM_BYTES * 3 // 4


def solution(mesh):
    def layer(*arrays):
        if fits_in_vmem(mesh, arrays):
            body = functools.partial(per_device_ring, arrays[7].shape[0])
        else:
            body = per_device_routed
        return mapped(body)(*arrays)

    def mapped(body):
        return jax.shard_map(
            body,
            mesh=mesh,
            in_specs=(
                P(("groups", "expert"), "seq", None),
                P(("groups", "expert"), "seq", None),
                P(("groups", "expert"), "seq", None),
                P(),
                P(),
                P(("groups", "expert"), "seq", None),
                P(("groups", "expert"), "seq", None),
                P(("seq", "expert"), None, None),
                P(("seq", "expert"), None, None),
                P(("seq", "expert"), None, None),
            ),
            out_specs=(P(("groups", "expert"), "seq", None), P(("groups", "expert"), "seq", None)),
            check_vma=False,
        )

    return layer
```

```python
import functools

import jax
import jax.numpy as jnp
from jax import lax
from jax.experimental import pallas as pl
from jax.experimental.pallas import tpu as pltpu
from jax.sharding import PartitionSpec as P

HEADS = 16
HEAD_DIM = 128


highest = lax.Precision.HIGHEST
epsilon = 1e-06


def prefix(value, axis, join, neutral):
    count, mine = (lax.axis_size(axis), lax.axis_index(axis))
    pieces = lax.all_gather(value, axis)
    subtotal = jnp.full_like(value, 0) + jnp.asarray(neutral, value.dtype)

    def turn(position, subtotal):
        longer = join(subtotal, pieces[position])
        return jnp.where(position < mine, longer, subtotal)

    return lax.fori_loop(0, count - 1, turn, subtotal)


def add_states(earlier, later):
    return earlier + later


def run_expert(inputs, gate_weight, up_weight, down_weight):
    gate_part = jnp.dot(inputs, gate_weight, preferred_element_type=jnp.float32)
    up_part = jnp.dot(inputs, up_weight, preferred_element_type=jnp.float32)
    expert_hidden = (jax.nn.silu(gate_part) * up_part).astype(jnp.bfloat16)
    return jnp.dot(expert_hidden, down_weight, preferred_element_type=jnp.float32).astype(
        jnp.bfloat16
    )


def to_owners(send_slots):
    return lax.all_to_all(send_slots, ("seq", "expert"), split_axis=0, concat_axis=0, tiled=True)


def from_owners(result_slots):
    return lax.all_to_all(result_slots, ("seq", "expert"), split_axis=0, concat_axis=0, tiled=True)


def per_device_routed(
    queries,
    key_rows,
    value_rows,
    head_gain,
    ffn_gain,
    expert_ids,
    router_weight,
    w_gate,
    w_up,
    w_down,
):
    row_count = queries.shape[1]
    model_width = queries.shape[2]
    block_rows = min(row_count, 512)
    block_count = row_count // block_rows
    block_shape = (block_count, block_rows, HEADS, HEAD_DIM)
    query_blocks = queries.reshape(block_shape)
    key_blocks = key_rows.reshape(block_shape)
    value_blocks = value_rows.reshape(block_shape)
    block_states = jnp.einsum(
        "nthd,nthe->nhde", key_blocks, value_blocks, preferred_element_type=jnp.float32
    )
    local_state = jnp.sum(block_states, axis=0)
    carried = prefix(local_state, "seq", add_states, jnp.zeros_like(local_state))
    starts = carried[None] + jnp.cumsum(block_states, axis=0) - block_states
    causal = jnp.arange(block_rows)[:, None] >= jnp.arange(block_rows)[None, :]
    scores = jnp.einsum(
        "nthd,nuhd->nhtu", query_blocks, key_blocks, preferred_element_type=jnp.float32
    )
    scores = jnp.where(causal, scores, 0.0)
    within = jnp.einsum(
        "nhtu,nuhe->nthe", scores, value_blocks.astype(jnp.float32), precision=highest
    )
    before = jnp.einsum(
        "nthd,nhde->nthe", query_blocks.astype(jnp.float32), starts, precision=highest
    )
    heads_raw = (within + before).reshape(row_count, HEADS, HEAD_DIM)
    mean_square = jnp.mean(heads_raw * heads_raw, axis=-1, keepdims=True)
    attention = (
        (heads_raw * lax.rsqrt(mean_square + epsilon)).reshape(row_count, model_width) * head_gain
    ).astype(jnp.bfloat16)
    attn_float = attention.astype(jnp.float32)
    feature_sq = jnp.mean(attn_float * attn_float, axis=-1, keepdims=True)
    normed = (attn_float * lax.rsqrt(feature_sq + epsilon) * ffn_gain).astype(jnp.bfloat16)
    top_count = expert_ids.shape[2]
    owners = lax.axis_size("seq") * lax.axis_size("expert")
    capacity = min(row_count, 3 * row_count * top_count // (2 * owners))
    slot_total = owners * capacity
    route_flat = expert_ids.reshape(row_count * top_count)
    onehot = (route_flat[:, None] == jnp.arange(owners, dtype=jnp.int32)[None, :]).astype(jnp.int32)
    position = jnp.sum(jnp.cumsum(onehot, axis=0) * onehot, axis=1) - 1
    destination = route_flat * capacity + position
    token_order = jnp.arange(row_count * top_count, dtype=jnp.int32) // top_count
    slot_token = jnp.full((slot_total,), row_count, jnp.int32).at[destination].set(token_order)
    send_slots = jnp.take(normed, slot_token, axis=0, mode="fill", fill_value=0).reshape(
        owners, capacity, model_width
    )
    received = to_owners(send_slots).reshape(slot_total, model_width)
    computed = run_expert(received, w_gate[0], w_up[0], w_down[0])
    returned = from_owners(computed.reshape(owners, capacity, model_width)).reshape(
        slot_total, model_width
    )
    picked = jnp.take(returned, destination, axis=0).reshape(row_count, top_count, model_width)
    shares = router_weight[0] / jnp.sum(router_weight[0], axis=-1, keepdims=True)
    mixture = jnp.einsum("tk,tkd->td", shares, picked.astype(jnp.float32), precision=highest)
    layer_out = (attn_float + mixture).astype(jnp.bfloat16)
    return (
        attention.reshape(1, row_count, model_width),
        layer_out.reshape(1, row_count, model_width),
    )


MESH = pl.DeviceIdType.MESH
VMEM_BYTES = 58 * 1024 * 1024
SCAN_PARTS = 4
ROW_PARTS = 4


def layer_kernel(
    count,
    q_hbm, k_hbm, v_hbm, head_gain, ffn_gain, ids_ref, score_ref, wg_ref, wu_ref, wd_ref,
    att_ref, mix_ref,
    q_ref, k_ref, v_ref, w_in, w_out, gates, rows, normed, partial, hidden, share, state, within,
    a_out, a_in, c_out, c_in, b_out, b_in, sum_in, sum_out,
    in_sem, w_sem, w_send, w_recv, gate_send, gate_recv, a_send, a_recv, c_send, c_recv, b_send, b_recv,
    row_send, row_recv, sum_send, sum_recv,
):
    half_ring = count // 2
    group = lax.axis_index("groups")
    me = lax.axis_index("seq")
    core = lax.axis_index("expert")
    z, y = me // 2, me % 2
    ring = jnp.where(y == 0, z, count - 1 - z)

    def at_ring(place):
        place = lax.rem(place + 2 * count, count)
        seq = jnp.where(place < half_ring, 2 * place, 2 * (count - 1 - place) + 1)
        return (group, seq, core)

    right, left = at_ring(ring + 1), at_ring(ring - 1)
    sibling = (group, me, 1 - core)
    tokens, width = q_ref.shape
    low = tokens // 2
    ff = wg_ref.shape[2]
    part = HEADS // SCAN_PARTS

    barrier = pltpu.get_barrier_semaphore()
    for d in range(1, count):
        pl.semaphore_signal(barrier, inc=1, device_id=at_ring(ring + d), device_id_type=MESH)
    pl.semaphore_signal(barrier, inc=1, device_id=sibling, device_id_type=MESH)

    in_copies = [
        pltpu.make_async_copy(k_hbm, k_ref, in_sem.at[0]),
        pltpu.make_async_copy(v_hbm, v_ref, in_sem.at[1]),
        pltpu.make_async_copy(q_hbm, q_ref, in_sem.at[2]),
    ]
    for c in in_copies:
        c.start()
    own_copies = [
        pltpu.make_async_copy(wg_ref.at[0], w_in.at[0], w_sem.at[0]),
        pltpu.make_async_copy(wu_ref.at[0], w_in.at[1], w_sem.at[1]),
        pltpu.make_async_copy(wd_ref.at[0], w_out.at[0], w_sem.at[2]),
    ]
    for c in own_copies:
        c.start()

    def head(h):
        return pl.ds(h * HEAD_DIM, HEAD_DIM)

    half_rows = HEADS * HEAD_DIM // 2
    piece = half_rows // SCAN_PARTS
    mine, other = y * half_rows, (1 - y) * half_rows

    def head_state(base, h):
        cols = pl.ds(pl.multiple_of(base + h * HEAD_DIM, HEAD_DIM), HEAD_DIM)
        return lax.dot_general(
            k_ref[:, cols], v_ref[:, cols], (((0,), (0,)), ((), ())),
            preferred_element_type=jnp.float32,
        )

    for c in in_copies[:2]:
        c.wait()
    for h in range(HEADS // 2):
        a_out[head(h), :] = head_state(other, h).astype(jnp.bfloat16)

    pl.semaphore_wait(barrier, count)

    def remote(src, dst, send, recv, where):
        return pltpu.make_async_remote_copy(
            src_ref=src, dst_ref=dst, send_sem=send, recv_sem=recv,
            device_id=where, device_id_type=MESH,
        )

    across = (group, me + 1 - 2 * y, core)
    above = (group, lax.rem(me + 2, count), core)

    def span(j):
        return pl.ds(j * piece, piece)

    def a_copy(j):
        return remote(a_out.at[span(j)], a_in.at[span(j)], a_send.at[j], a_recv.at[j], across)

    def b_copy(j):
        return remote(b_out.at[span(j)], b_in.at[span(j)], b_send.at[j], b_recv.at[j], across)

    def c_copy(j):
        return remote(c_out.at[span(j)], c_in.at[span(j)], c_send.at[j], c_recv.at[j], above)

    for j in range(SCAN_PARTS):
        a_copy(j).start()
    for h in range(HEADS // 2):
        state[head(h), :] = head_state(mine, h)
    in_copies[2].wait()

    gate_rows = gates.shape[2] - 8
    picks = lax.broadcasted_iota(jnp.int32, (gate_rows, tokens), 0)
    scores = score_ref[...]
    named = scores / jnp.sum(scores, axis=0, keepdims=True)
    ids = ids_ref[...]
    dense = jnp.zeros((gate_rows, tokens), jnp.float32)
    for t in range(ids.shape[0]):
        dense += jnp.where(ids[t : t + 1, :] == picks, named[t : t + 1, :], 0.0)
    gates[0, 0, pl.ds(0, gate_rows), :] = dense

    causal = lax.broadcasted_iota(jnp.int32, (tokens, tokens), 0) >= lax.broadcasted_iota(
        jnp.int32, (tokens, tokens), 1
    )
    for h in range(HEADS):
        pair = lax.dot_general(
            q_ref[:, head(h)], k_ref[:, head(h)], (((1,), (1,)), ((), ())),
            preferred_element_type=jnp.float32,
        )
        pair = jnp.where(causal, pair, 0.0).astype(jnp.bfloat16)
        within[:, head(h)] = jnp.dot(pair, v_ref[:, head(h)], preferred_element_type=jnp.float32)

    for j in range(SCAN_PARTS):
        a_copy(j).wait_recv()

        @pl.when(z == 0)
        def _():
            c_in[span(j), :] = jnp.zeros((piece, HEAD_DIM), jnp.bfloat16)

        @pl.when(z > 0)
        def _():
            c_copy(j).wait_recv()

        earlier = c_in[span(j), :].astype(jnp.float32)
        own = state[span(j), :]
        c_out[span(j), :] = (
            earlier + (own + a_in[span(j), :].astype(jnp.float32))
        ).astype(jnp.bfloat16)

        @pl.when(z < half_ring - 1)
        def _():
            c_copy(j).start()

        b_out[span(j), :] = (earlier + jnp.where(y == 0, own, 0.0)).astype(jnp.bfloat16)
        b_copy(j).start()

    weight_copies = [
        remote(wg_ref.at[0], w_in.at[2], w_send.at[0], w_recv.at[0], sibling),
        remote(wu_ref.at[0], w_in.at[3], w_send.at[1], w_recv.at[1], sibling),
        remote(wd_ref.at[0], w_out.at[1], w_send.at[2], w_recv.at[2], sibling),
    ]

    part_width = width // ROW_PARTS

    def row_copy(side, step, i, origin):
        place = lax.rem(origin + 2 * count, count)
        first = jnp.where(place < half_ring, 0, ROW_PARTS // 2)
        c = lax.rem(first + i, ROW_PARTS)
        cols = pl.ds(pl.multiple_of(c * part_width, part_width), part_width)
        src = rows.at[step - 1, pl.ds(0 if step == 1 else side * tokens, tokens), cols]
        if step < half_ring:
            dst = rows.at[step, pl.ds(side * tokens, tokens), cols]
        else:
            dst = rows.at[0, pl.ds(tokens, tokens), cols]
        return remote(
            src, dst, row_send.at[side, step - 1, i], row_recv.at[side, step - 1, i],
            right if side == 0 else left,
        )

    def row_out(side, step, i):
        back = step - 1
        return row_copy(side, step, i, ring - back if side == 0 else ring + back)

    def row_arrival(side, step, i):
        return row_copy(side, step, i, ring - step if side == 0 else ring + step)

    def goes(side, step, i):
        return step < half_ring or (i < ROW_PARTS // 2) == (side == 0)

    square = jnp.zeros((tokens, HEAD_DIM), jnp.float32)
    heads_each = piece // HEAD_DIM
    for j in range(2 * SCAN_PARTS):
        if j < SCAN_PARTS:
            base, k = mine, j
            start = c_in[span(k), :].astype(jnp.float32) + jnp.where(
                y == 1, a_in[span(k), :].astype(jnp.float32), 0.0
            )
            start = start.astype(jnp.bfloat16)
        else:
            base, k = other, j - SCAN_PARTS
            b_copy(k).wait_recv()
            start = b_in[span(k), :]
        for i in range(heads_each):
            cols = pl.ds(
                pl.multiple_of(base + k * piece + i * HEAD_DIM, HEAD_DIM), HEAD_DIM
            )
            raw = within[:, cols] + jnp.dot(
                q_ref[:, cols], start[i * HEAD_DIM : (i + 1) * HEAD_DIM],
                preferred_element_type=jnp.float32,
            )
            mean_square = jnp.mean(raw * raw, axis=-1, keepdims=True)
            att = (raw * lax.rsqrt(mean_square + epsilon) * head_gain[:, cols]).astype(
                jnp.bfloat16
            )
            rows[0, pl.ds(0, tokens), cols] = att
            att = att.astype(jnp.float32)
            att_ref[:, cols] = att
            square += att * att
        if (j + 1) % (2 * SCAN_PARTS // ROW_PARTS) == 0:
            for side in range(2):
                row_out(side, 1, j // (2 * SCAN_PARTS // ROW_PARTS)).start()
        if j < len(weight_copies):
            weight_copies[j].start()

    scale = lax.rsqrt(jnp.sum(jnp.transpose(square), axis=0, keepdims=True) / width + epsilon)
    gates[0, 0, pl.ds(gate_rows, 8), :] = jnp.broadcast_to(scale, (8, tokens))
    gate_copies = []
    for d in range(1, count):
        slot = (d, 0) if d < half_ring else ((0, 1) if d == half_ring else (count - d, 1))
        gate_copies.append(
            remote(gates.at[0, 0], gates.at[slot[0], slot[1]],
                   gate_send.at[slot[0], slot[1]], gate_recv.at[slot[0], slot[1]],
                   at_ring(ring + d))
        )
    for c in gate_copies:
        c.start()

    def row_span(side, h):
        return pl.ds(side * tokens + h * low, low)

    tile = 256

    def expert_pieces(index, first, size):
        here = pl.ds(first, size)

        def norm():
            line = lax.broadcasted_iota(jnp.int32, (gate_rows + 8, 128), 0)
            for e, owner in enumerate((2 * me + core, 2 * me + 1 - core, gate_rows)):
                chosen = (line == owner).astype(jnp.float32)
                for side in range(first // tokens, (first + size) // tokens):
                    share[e, pl.ds(side * tokens, tokens), :] = lax.dot_general(
                        gates[index, side], chosen, (((0,), (0,)), ((), ())),
                        preferred_element_type=jnp.float32, precision=highest,
                    )

            @pl.loop(0, width // tile)
            def _(n):
                cols = pl.ds(pl.multiple_of(n * tile, tile), tile)
                normed[here, cols] = (
                    rows[index, here, cols].astype(jnp.float32)
                    * share[2, here, 0:1]
                    * ffn_gain[:, cols]
                ).astype(jnp.bfloat16)

        def into_hidden(e):
            @pl.loop(0, ff // tile)
            def _(n):
                cols = pl.ds(pl.multiple_of(n * tile, tile), tile)
                x = normed[here, :]
                gate_part = jnp.dot(
                    x, w_in[2 * e, :, cols], preferred_element_type=jnp.float32
                )
                up_part = jnp.dot(
                    x, w_in[2 * e + 1, :, cols], preferred_element_type=jnp.float32
                )
                act = gate_part / (1.0 + jnp.exp(-gate_part)) * up_part
                hidden[here, pl.ds(pl.multiple_of(e * ff + n * tile, tile), tile)] = (
                    act * share[e, here, 0:1]
                ).astype(jnp.bfloat16)

        def from_hidden():
            @pl.loop(0, width // tile)
            def _(n):
                cols = pl.ds(pl.multiple_of(n * tile, tile), tile)
                partial[index, here, cols] = jnp.dot(
                    hidden[here, pl.ds(0, ff)], w_out[0, :, cols],
                    preferred_element_type=jnp.float32,
                ) + jnp.dot(
                    hidden[here, pl.ds(ff, ff)], w_out[1, :, cols],
                    preferred_element_type=jnp.float32,
                )

        return [
            norm,
            functools.partial(into_hidden, 0),
            functools.partial(into_hidden, 1),
            from_hidden,
        ]

    def sum_copy(side, step, h):
        here = (side, step - 1, pl.ds(h * low, low))
        return remote(
            sum_out.at[here], sum_in.at[here],
            sum_send.at[side, step - 1, h], sum_recv.at[side, step - 1, h],
            right if side == 0 else left,
        )

    def sum_step(side, step, h):
        index = half_ring - step + 1 if step > 1 else 0
        value = partial[index, row_span(1 if step == 1 else 1 - side, h), :]
        if step > 2 or (step == 2 and h == side):
            sum_copy(side, step - 1, h).wait_recv()
            value += sum_in[side, step - 2, pl.ds(h * low, low), :].astype(jnp.float32)
        sum_out[side, step - 1, pl.ds(h * low, low), :] = value.astype(jnp.bfloat16)
        sum_copy(side, step, h).start()

    def take(step, i):
        for side in range(2):
            if goes(side, step, i):
                row_arrival(side, step, i).wait_recv()
            if step < half_ring and goes(side, step + 1, i):
                row_out(side, step + 1, i).start()

    for i in range(ROW_PARTS):
        take(1, i)
    for c in own_copies:
        c.wait()
    for c in weight_copies:
        c.wait_recv()
    for c in gate_copies:
        c.wait_recv()
    for step in range(1, half_ring):
        for i, work in enumerate(expert_pieces(step, 0, 2 * tokens)):
            if step + 1 < half_ring:
                take(step + 1, i)
            work()
    for side in range(2):
        sum_step(side, 2, 1 - side)
    for i in range(ROW_PARTS):
        take(half_ring, i)
    for work in expert_pieces(0, tokens, tokens):
        work()
    for side in range(2):
        sum_step(side, 1, side)
    for work in expert_pieces(0, 0, tokens):
        work()
    for side in range(2):
        sum_step(side, 2, side)
    for step in range(3, half_ring + 1):
        for first in range(2):
            for side in range(2):
                sum_step(side, step, (1 - side + first) % 2)
    for h in range(2):
        total = partial[0, row_span(0, h), :]
        for side in range(2):
            sum_copy(side, half_ring, h).wait_recv()
            total += sum_in[side, half_ring - 1, pl.ds(h * low, low), :].astype(jnp.float32)
        mix_ref[pl.ds(h * low, low), :] = total

    for c in weight_copies + gate_copies:
        c.wait_send()
    for j in range(SCAN_PARTS):
        @pl.when(z < half_ring - 1)
        def _():
            c_copy(j).wait_send()

        a_copy(j).wait_send()
        b_copy(j).wait_send()
    for side in range(2):
        for step in range(1, half_ring + 1):
            for i in range(ROW_PARTS):
                if goes(side, step, i):
                    row_out(side, step, i).wait_send()
            for h in range(2):
                if step > 1 or h == side:
                    sum_copy(side, step, h).wait_send()


def per_device_ring(
    experts,
    queries,
    key_rows,
    value_rows,
    head_gain,
    ffn_gain,
    expert_ids,
    router_weight,
    w_gate,
    w_up,
    w_down,
):
    count = lax.axis_size("seq")
    half_ring = count // 2
    tokens, width = queries.shape[1:]
    ff = w_gate.shape[2]
    bf16, f32 = jnp.bfloat16, jnp.float32
    vmem = pl.BlockSpec(memory_space=pltpu.VMEM)
    hbm = pl.BlockSpec(memory_space=pl.ANY)
    dma = pltpu.SemaphoreType.DMA
    half_states = (HEADS * HEAD_DIM // 2, HEAD_DIM)
    gate_rows = -(-experts // 8) * 8 + 8
    attention, mixture = pl.pallas_call(
        functools.partial(layer_kernel, count),
        out_shape=[jax.ShapeDtypeStruct((tokens, width), f32)] * 2,
        in_specs=[hbm] * 3 + [vmem] * 4 + [hbm] * 3,
        out_specs=[vmem] * 2,
        scratch_shapes=[
            pltpu.VMEM((tokens, width), bf16),
            pltpu.VMEM((tokens, width), bf16),
            pltpu.VMEM((tokens, width), bf16),
            pltpu.VMEM((4, width, ff), bf16),
            pltpu.VMEM((2, ff, width), bf16),
            pltpu.VMEM((half_ring, 2, gate_rows, tokens), f32),
            pltpu.VMEM((half_ring, 2 * tokens, width), bf16),
            pltpu.VMEM((2 * tokens, width), bf16),
            pltpu.VMEM((half_ring, 2 * tokens, width), f32),
            pltpu.VMEM((2 * tokens, 2 * ff), bf16),
            pltpu.VMEM((3, 2 * tokens, 128), f32),
            pltpu.VMEM(half_states, f32),
            pltpu.VMEM((tokens, width), f32),
            pltpu.VMEM(half_states, bf16),
            pltpu.VMEM(half_states, bf16),
            pltpu.VMEM(half_states, bf16),
            pltpu.VMEM(half_states, bf16),
            pltpu.VMEM(half_states, bf16),
            pltpu.VMEM(half_states, bf16),
            pltpu.VMEM((2, half_ring, tokens, width), bf16),
            pltpu.VMEM((2, half_ring, tokens, width), bf16),
            dma((3,)),
            dma((3,)),
            dma((3,)),
            dma((3,)),
            dma((half_ring, 2)),
            dma((half_ring, 2)),
            dma((SCAN_PARTS,)),
            dma((SCAN_PARTS,)),
            dma((SCAN_PARTS,)),
            dma((SCAN_PARTS,)),
            dma((SCAN_PARTS,)),
            dma((SCAN_PARTS,)),
            dma((2, half_ring, ROW_PARTS)),
            dma((2, half_ring, ROW_PARTS)),
            dma((2, half_ring, 2)),
            dma((2, half_ring, 2)),
        ],
        compiler_params=pltpu.CompilerParams(
            collective_id=0, has_side_effects=True, vmem_limit_bytes=VMEM_BYTES
        ),
        cost_estimate=pl.CostEstimate(
            flops=12 * count * tokens * width * ff,
            bytes_accessed=6 * width * ff + 10 * tokens * width,
            transcendentals=2 * count * tokens * ff,
        ),
    )(
        queries[0],
        key_rows[0],
        value_rows[0],
        head_gain.reshape(1, width),
        ffn_gain.reshape(1, width),
        expert_ids[0].T,
        router_weight[0].T,
        w_gate,
        w_up,
        w_down,
    )
    layer_out = attention + mixture
    return attention.astype(bf16)[None], layer_out.astype(bf16)[None]


def fits_in_vmem(mesh, arrays):
    count = mesh.shape["seq"]
    queries, w_gate = arrays[0], arrays[7]
    tokens, width = queries.shape[1] // count, queries.shape[2]
    held = count * tokens * width * (2 + 4 + 2 + 2) + 12 * width * w_gate.shape[2]
    return held < VMEM_BYTES * 3 // 4


def solution(mesh):
    def layer(*arrays):
        if fits_in_vmem(mesh, arrays):
            body = functools.partial(per_device_ring, arrays[7].shape[0])
        else:
            body = per_device_routed
        return mapped(body)(*arrays)

    def mapped(body):
        return jax.shard_map(
            body,
            mesh=mesh,
            in_specs=(
                P(("groups", "expert"), "seq", None),
                P(("groups", "expert"), "seq", None),
                P(("groups", "expert"), "seq", None),
                P(),
                P(),
                P(("groups", "expert"), "seq", None),
                P(("groups", "expert"), "seq", None),
                P(("seq", "expert"), None, None),
                P(("seq", "expert"), None, None),
                P(("seq", "expert"), None, None),
            ),
            out_specs=(P(("groups", "expert"), "seq", None), P(("groups", "expert"), "seq", None)),
            check_vma=False,
        )

    return layer
```

```python
import functools

import jax
import jax.numpy as jnp
from jax import lax
from jax.experimental import pallas as pl
from jax.experimental.pallas import tpu as pltpu
from jax.sharding import PartitionSpec as P

HEADS = 16
HEAD_DIM = 128


highest = lax.Precision.HIGHEST
epsilon = 1e-06


def prefix(value, axis, join, neutral):
    count, mine = (lax.axis_size(axis), lax.axis_index(axis))
    pieces = lax.all_gather(value, axis)
    subtotal = jnp.full_like(value, 0) + jnp.asarray(neutral, value.dtype)

    def turn(position, subtotal):
        longer = join(subtotal, pieces[position])
        return jnp.where(position < mine, longer, subtotal)

    return lax.fori_loop(0, count - 1, turn, subtotal)


def add_states(earlier, later):
    return earlier + later


def run_expert(inputs, gate_weight, up_weight, down_weight):
    gate_part = jnp.dot(inputs, gate_weight, preferred_element_type=jnp.float32)
    up_part = jnp.dot(inputs, up_weight, preferred_element_type=jnp.float32)
    expert_hidden = (jax.nn.silu(gate_part) * up_part).astype(jnp.bfloat16)
    return jnp.dot(expert_hidden, down_weight, preferred_element_type=jnp.float32).astype(
        jnp.bfloat16
    )


def to_owners(send_slots):
    return lax.all_to_all(send_slots, ("seq", "expert"), split_axis=0, concat_axis=0, tiled=True)


def from_owners(result_slots):
    return lax.all_to_all(result_slots, ("seq", "expert"), split_axis=0, concat_axis=0, tiled=True)


def per_device_routed(
    queries,
    key_rows,
    value_rows,
    head_gain,
    ffn_gain,
    expert_ids,
    router_weight,
    w_gate,
    w_up,
    w_down,
):
    row_count = queries.shape[1]
    model_width = queries.shape[2]
    block_rows = min(row_count, 512)
    block_count = row_count // block_rows
    block_shape = (block_count, block_rows, HEADS, HEAD_DIM)
    query_blocks = queries.reshape(block_shape)
    key_blocks = key_rows.reshape(block_shape)
    value_blocks = value_rows.reshape(block_shape)
    block_states = jnp.einsum(
        "nthd,nthe->nhde", key_blocks, value_blocks, preferred_element_type=jnp.float32
    )
    local_state = jnp.sum(block_states, axis=0)
    carried = prefix(local_state, "seq", add_states, jnp.zeros_like(local_state))
    starts = carried[None] + jnp.cumsum(block_states, axis=0) - block_states
    causal = jnp.arange(block_rows)[:, None] >= jnp.arange(block_rows)[None, :]
    scores = jnp.einsum(
        "nthd,nuhd->nhtu", query_blocks, key_blocks, preferred_element_type=jnp.float32
    )
    scores = jnp.where(causal, scores, 0.0)
    within = jnp.einsum(
        "nhtu,nuhe->nthe", scores, value_blocks.astype(jnp.float32), precision=highest
    )
    before = jnp.einsum(
        "nthd,nhde->nthe", query_blocks.astype(jnp.float32), starts, precision=highest
    )
    heads_raw = (within + before).reshape(row_count, HEADS, HEAD_DIM)
    mean_square = jnp.mean(heads_raw * heads_raw, axis=-1, keepdims=True)
    attention = (
        (heads_raw * lax.rsqrt(mean_square + epsilon)).reshape(row_count, model_width) * head_gain
    ).astype(jnp.bfloat16)
    attn_float = attention.astype(jnp.float32)
    feature_sq = jnp.mean(attn_float * attn_float, axis=-1, keepdims=True)
    normed = (attn_float * lax.rsqrt(feature_sq + epsilon) * ffn_gain).astype(jnp.bfloat16)
    top_count = expert_ids.shape[2]
    owners = lax.axis_size("seq") * lax.axis_size("expert")
    capacity = min(row_count, 3 * row_count * top_count // (2 * owners))
    slot_total = owners * capacity
    route_flat = expert_ids.reshape(row_count * top_count)
    onehot = (route_flat[:, None] == jnp.arange(owners, dtype=jnp.int32)[None, :]).astype(jnp.int32)
    position = jnp.sum(jnp.cumsum(onehot, axis=0) * onehot, axis=1) - 1
    destination = route_flat * capacity + position
    token_order = jnp.arange(row_count * top_count, dtype=jnp.int32) // top_count
    slot_token = jnp.full((slot_total,), row_count, jnp.int32).at[destination].set(token_order)
    send_slots = jnp.take(normed, slot_token, axis=0, mode="fill", fill_value=0).reshape(
        owners, capacity, model_width
    )
    received = to_owners(send_slots).reshape(slot_total, model_width)
    computed = run_expert(received, w_gate[0], w_up[0], w_down[0])
    returned = from_owners(computed.reshape(owners, capacity, model_width)).reshape(
        slot_total, model_width
    )
    picked = jnp.take(returned, destination, axis=0).reshape(row_count, top_count, model_width)
    shares = router_weight[0] / jnp.sum(router_weight[0], axis=-1, keepdims=True)
    mixture = jnp.einsum("tk,tkd->td", shares, picked.astype(jnp.float32), precision=highest)
    layer_out = (attn_float + mixture).astype(jnp.bfloat16)
    return (
        attention.reshape(1, row_count, model_width),
        layer_out.reshape(1, row_count, model_width),
    )


MESH = pl.DeviceIdType.MESH
VMEM_BYTES = 58 * 1024 * 1024
SCAN_PARTS = 4
ROW_PARTS = 4


def layer_kernel(
    count,
    q_hbm, k_hbm, v_hbm, head_gain, ffn_gain, ids_ref, score_ref, wg_ref, wu_ref, wd_ref,
    att_ref, mix_ref,
    q_ref, k_ref, v_ref, w_in, w_out, gates, rows, normed, partial, hidden, share, state, within,
    a_out, a_in, c_out, c_in, b_out, b_in, sum_in, sum_out,
    in_sem, w_sem, w_send, w_recv, gate_send, gate_recv, a_send, a_recv, c_send, c_recv, b_send, b_recv,
    row_send, row_recv, sum_send, sum_recv,
):
    half_ring = count // 2
    group = lax.axis_index("groups")
    me = lax.axis_index("seq")
    core = lax.axis_index("expert")
    z, y = me // 2, me % 2
    ring = jnp.where(y == 0, z, count - 1 - z)

    def at_ring(place):
        place = lax.rem(place + 2 * count, count)
        seq = jnp.where(place < half_ring, 2 * place, 2 * (count - 1 - place) + 1)
        return (group, seq, core)

    right, left = at_ring(ring + 1), at_ring(ring - 1)
    sibling = (group, me, 1 - core)
    tokens, width = q_ref.shape
    low = tokens // 2
    ff = wg_ref.shape[2]
    part = HEADS // SCAN_PARTS

    barrier = pltpu.get_barrier_semaphore()
    for d in range(1, count):
        pl.semaphore_signal(barrier, inc=1, device_id=at_ring(ring + d), device_id_type=MESH)
    pl.semaphore_signal(barrier, inc=1, device_id=sibling, device_id_type=MESH)

    in_copies = [
        pltpu.make_async_copy(k_hbm, k_ref, in_sem.at[0]),
        pltpu.make_async_copy(v_hbm, v_ref, in_sem.at[1]),
        pltpu.make_async_copy(q_hbm, q_ref, in_sem.at[2]),
    ]
    for c in in_copies:
        c.start()
    own_copies = [
        pltpu.make_async_copy(wg_ref.at[0], w_in.at[0], w_sem.at[0]),
        pltpu.make_async_copy(wu_ref.at[0], w_in.at[1], w_sem.at[1]),
        pltpu.make_async_copy(wd_ref.at[0], w_out.at[pl.ds(0, ff)], w_sem.at[2]),
    ]
    for c in own_copies:
        c.start()

    def head(h):
        return pl.ds(h * HEAD_DIM, HEAD_DIM)

    half_rows = HEADS * HEAD_DIM // 2
    piece = half_rows // SCAN_PARTS
    mine, other = y * half_rows, (1 - y) * half_rows

    def head_state(base, h):
        cols = pl.ds(pl.multiple_of(base + h * HEAD_DIM, HEAD_DIM), HEAD_DIM)
        return lax.dot_general(
            k_ref[:, cols], v_ref[:, cols], (((0,), (0,)), ((), ())),
            preferred_element_type=jnp.float32,
        )

    for c in in_copies[:2]:
        c.wait()
    for h in range(HEADS // 2):
        a_out[head(h), :] = head_state(other, h).astype(jnp.bfloat16)

    pl.semaphore_wait(barrier, count)

    def remote(src, dst, send, recv, where):
        return pltpu.make_async_remote_copy(
            src_ref=src, dst_ref=dst, send_sem=send, recv_sem=recv,
            device_id=where, device_id_type=MESH,
        )

    across = (group, me + 1 - 2 * y, core)
    above = (group, lax.rem(me + 2, count), core)

    def span(j):
        return pl.ds(j * piece, piece)

    def a_copy(j):
        return remote(a_out.at[span(j)], a_in.at[span(j)], a_send.at[j], a_recv.at[j], across)

    def b_copy(j):
        return remote(b_out.at[span(j)], b_in.at[span(j)], b_send.at[j], b_recv.at[j], across)

    def c_copy(j):
        return remote(c_out.at[span(j)], c_in.at[span(j)], c_send.at[j], c_recv.at[j], above)

    for j in range(SCAN_PARTS):
        a_copy(j).start()
    for h in range(HEADS // 2):
        state[head(h), :] = head_state(mine, h)
    in_copies[2].wait()

    gate_rows = gates.shape[2] - 8
    picks = lax.broadcasted_iota(jnp.int32, (gate_rows, tokens), 0)
    scores = score_ref[...]
    named = scores / jnp.sum(scores, axis=0, keepdims=True)
    ids = ids_ref[...]
    dense = jnp.zeros((gate_rows, tokens), jnp.float32)
    for t in range(ids.shape[0]):
        dense += jnp.where(ids[t : t + 1, :] == picks, named[t : t + 1, :], 0.0)
    gates[0, 0, pl.ds(0, gate_rows), :] = dense

    causal = lax.broadcasted_iota(jnp.int32, (tokens, tokens), 0) >= lax.broadcasted_iota(
        jnp.int32, (tokens, tokens), 1
    )
    for h in range(HEADS):
        pair = lax.dot_general(
            q_ref[:, head(h)], k_ref[:, head(h)], (((1,), (1,)), ((), ())),
            preferred_element_type=jnp.float32,
        )
        pair = jnp.where(causal, pair, 0.0).astype(jnp.bfloat16)
        within[:, head(h)] = jnp.dot(pair, v_ref[:, head(h)], preferred_element_type=jnp.float32)

    for j in range(SCAN_PARTS):
        a_copy(j).wait_recv()

        @pl.when(z == 0)
        def _():
            c_in[span(j), :] = jnp.zeros((piece, HEAD_DIM), jnp.bfloat16)

        @pl.when(z > 0)
        def _():
            c_copy(j).wait_recv()

        earlier = c_in[span(j), :].astype(jnp.float32)
        own = state[span(j), :]
        c_out[span(j), :] = (
            earlier + (own + a_in[span(j), :].astype(jnp.float32))
        ).astype(jnp.bfloat16)

        @pl.when(z < half_ring - 1)
        def _():
            c_copy(j).start()

        b_out[span(j), :] = (earlier + jnp.where(y == 0, own, 0.0)).astype(jnp.bfloat16)
        b_copy(j).start()

    weight_copies = [
        remote(wg_ref.at[0], w_in.at[2], w_send.at[0], w_recv.at[0], sibling),
        remote(wu_ref.at[0], w_in.at[3], w_send.at[1], w_recv.at[1], sibling),
        remote(wd_ref.at[0], w_out.at[pl.ds(ff, ff)], w_send.at[2], w_recv.at[2], sibling),
    ]

    part_width = width // ROW_PARTS

    def row_copy(side, step, i, origin):
        place = lax.rem(origin + 2 * count, count)
        first = jnp.where(place < half_ring, 0, ROW_PARTS // 2)
        c = lax.rem(first + i, ROW_PARTS)
        cols = pl.ds(pl.multiple_of(c * part_width, part_width), part_width)
        src = rows.at[step - 1, pl.ds(0 if step == 1 else side * tokens, tokens), cols]
        if step < half_ring:
            dst = rows.at[step, pl.ds(side * tokens, tokens), cols]
        else:
            dst = rows.at[0, pl.ds(tokens, tokens), cols]
        return remote(
            src, dst, row_send.at[side, step - 1, i], row_recv.at[side, step - 1, i],
            right if side == 0 else left,
        )

    def row_out(side, step, i):
        back = step - 1
        return row_copy(side, step, i, ring - back if side == 0 else ring + back)

    def row_arrival(side, step, i):
        return row_copy(side, step, i, ring - step if side == 0 else ring + step)

    def goes(side, step, i):
        return step < half_ring or (i < ROW_PARTS // 2) == (side == 0)

    square = jnp.zeros((tokens, HEAD_DIM), jnp.float32)
    heads_each = piece // HEAD_DIM
    for j in range(2 * SCAN_PARTS):
        if j < SCAN_PARTS:
            base, k = mine, j
            start = c_in[span(k), :].astype(jnp.float32) + jnp.where(
                y == 1, a_in[span(k), :].astype(jnp.float32), 0.0
            )
            start = start.astype(jnp.bfloat16)
        else:
            base, k = other, j - SCAN_PARTS
            b_copy(k).wait_recv()
            start = b_in[span(k), :]
        for i in range(heads_each):
            cols = pl.ds(
                pl.multiple_of(base + k * piece + i * HEAD_DIM, HEAD_DIM), HEAD_DIM
            )
            raw = within[:, cols] + jnp.dot(
                q_ref[:, cols], start[i * HEAD_DIM : (i + 1) * HEAD_DIM],
                preferred_element_type=jnp.float32,
            )
            mean_square = jnp.mean(raw * raw, axis=-1, keepdims=True)
            att = (raw * lax.rsqrt(mean_square + epsilon) * head_gain[:, cols]).astype(
                jnp.bfloat16
            )
            rows[0, pl.ds(0, tokens), cols] = att
            att = att.astype(jnp.float32)
            att_ref[:, cols] = att
            square += att * att
        if (j + 1) % (2 * SCAN_PARTS // ROW_PARTS) == 0:
            for side in range(2):
                row_out(side, 1, j // (2 * SCAN_PARTS // ROW_PARTS)).start()
        if j < len(weight_copies):
            weight_copies[j].start()

    scale = lax.rsqrt(jnp.sum(jnp.transpose(square), axis=0, keepdims=True) / width + epsilon)
    gates[0, 0, pl.ds(gate_rows, 8), :] = jnp.broadcast_to(scale, (8, tokens))
    gate_copies = []
    for d in range(1, count):
        slot = (d, 0) if d < half_ring else ((0, 1) if d == half_ring else (count - d, 1))
        gate_copies.append(
            remote(gates.at[0, 0], gates.at[slot[0], slot[1]],
                   gate_send.at[slot[0], slot[1]], gate_recv.at[slot[0], slot[1]],
                   at_ring(ring + d))
        )
    for c in gate_copies:
        c.start()

    def row_span(side, h):
        return pl.ds(side * tokens + h * low, low)

    def expert_pieces(index, first, size):
        here = pl.ds(first, size)

        def norm():
            scale = share[index, here, 2:3]
            for h in range(HEADS):
                normed[here, head(h)] = (
                    rows[index, here, head(h)].astype(jnp.float32) * scale * ffn_gain[:, head(h)]
                ).astype(jnp.bfloat16)

        def into_hidden(e):
            x = normed[here, :]
            gate_part = jnp.dot(x, w_in[2 * e], preferred_element_type=jnp.float32)
            up_part = jnp.dot(x, w_in[2 * e + 1], preferred_element_type=jnp.float32)
            act = gate_part / (1.0 + jnp.exp(-gate_part)) * up_part
            hidden[here, pl.ds(e * ff, ff)] = (
                act * share[index, here, e : e + 1]
            ).astype(jnp.bfloat16)

        def from_hidden():
            partial[index, here, :] = jnp.dot(
                hidden[here, :], w_out[...], preferred_element_type=jnp.float32
            )

        return [
            norm,
            functools.partial(into_hidden, 0),
            functools.partial(into_hidden, 1),
            from_hidden,
        ]

    def sum_copy(side, step, h):
        here = (side, step - 1, pl.ds(h * low, low))
        return remote(
            sum_out.at[here], sum_in.at[here],
            sum_send.at[side, step - 1, h], sum_recv.at[side, step - 1, h],
            right if side == 0 else left,
        )

    def sum_step(side, step, h):
        index = half_ring - step + 1 if step > 1 else 0
        value = partial[index, row_span(1 if step == 1 else 1 - side, h), :]
        if step > 2 or (step == 2 and h == side):
            sum_copy(side, step - 1, h).wait_recv()
            value += sum_in[side, step - 2, pl.ds(h * low, low), :].astype(jnp.float32)
        sum_out[side, step - 1, pl.ds(h * low, low), :] = value.astype(jnp.bfloat16)
        sum_copy(side, step, h).start()

    def take(step, i):
        for side in range(2):
            if goes(side, step, i):
                row_arrival(side, step, i).wait_recv()
            if step < half_ring and goes(side, step + 1, i):
                row_out(side, step + 1, i).start()

    for i in range(ROW_PARTS):
        take(1, i)
    for c in own_copies:
        c.wait()
    for c in weight_copies:
        c.wait_recv()
    for c in gate_copies:
        c.wait_recv()
    line = lax.broadcasted_iota(jnp.int32, (gate_rows + 8, 128), 0)
    lane = lax.broadcasted_iota(jnp.int32, (gate_rows + 8, 128), 1)
    wanted = jnp.where(lane == 0, 2 * me + core, jnp.where(lane == 1, 2 * me + 1 - core, gate_rows))
    chosen = ((line == wanted) & (lane < 3)).astype(jnp.float32)
    for index in range(half_ring):
        for side in range(2):
            share[index, pl.ds(side * tokens, tokens), :] = lax.dot_general(
                gates[index, side], chosen, (((0,), (0,)), ((), ())),
                preferred_element_type=jnp.float32, precision=highest,
            )
    for step in range(1, half_ring):
        for i, work in enumerate(expert_pieces(step, 0, 2 * tokens)):
            if step + 1 < half_ring:
                take(step + 1, i)
            work()
    for side in range(2):
        sum_step(side, 2, 1 - side)
    for i in range(ROW_PARTS):
        take(half_ring, i)
    for work in expert_pieces(0, tokens, tokens):
        work()
    for side in range(2):
        sum_step(side, 1, side)
    later = [(step, first) for step in range(2, half_ring + 1) for first in range(2)][1:]
    own_work = expert_pieces(0, 0, tokens)
    for step, first in later:
        for side in range(2):
            sum_step(side, step, (1 - side + first) % 2)
        if own_work:
            own_work.pop(0)()
    for work in own_work:
        work()
    for h in range(2):
        total = partial[0, row_span(0, h), :]
        for side in range(2):
            sum_copy(side, half_ring, h).wait_recv()
            total += sum_in[side, half_ring - 1, pl.ds(h * low, low), :].astype(jnp.float32)
        mix_ref[pl.ds(h * low, low), :] = total

    for c in weight_copies + gate_copies:
        c.wait_send()
    for j in range(SCAN_PARTS):
        @pl.when(z < half_ring - 1)
        def _():
            c_copy(j).wait_send()

        a_copy(j).wait_send()
        b_copy(j).wait_send()
    for side in range(2):
        for step in range(1, half_ring + 1):
            for i in range(ROW_PARTS):
                if goes(side, step, i):
                    row_out(side, step, i).wait_send()
            for h in range(2):
                if step > 1 or h == side:
                    sum_copy(side, step, h).wait_send()


def per_device_ring(
    experts,
    queries,
    key_rows,
    value_rows,
    head_gain,
    ffn_gain,
    expert_ids,
    router_weight,
    w_gate,
    w_up,
    w_down,
):
    count = lax.axis_size("seq")
    half_ring = count // 2
    tokens, width = queries.shape[1:]
    ff = w_gate.shape[2]
    bf16, f32 = jnp.bfloat16, jnp.float32
    vmem = pl.BlockSpec(memory_space=pltpu.VMEM)
    hbm = pl.BlockSpec(memory_space=pl.ANY)
    dma = pltpu.SemaphoreType.DMA
    half_states = (HEADS * HEAD_DIM // 2, HEAD_DIM)
    gate_rows = -(-experts // 8) * 8 + 8
    attention, mixture = pl.pallas_call(
        functools.partial(layer_kernel, count),
        out_shape=[jax.ShapeDtypeStruct((tokens, width), f32)] * 2,
        in_specs=[hbm] * 3 + [vmem] * 4 + [hbm] * 3,
        out_specs=[vmem] * 2,
        scratch_shapes=[
            pltpu.VMEM((tokens, width), bf16),
            pltpu.VMEM((tokens, width), bf16),
            pltpu.VMEM((tokens, width), bf16),
            pltpu.VMEM((4, width, ff), bf16),
            pltpu.VMEM((2 * ff, width), bf16),
            pltpu.VMEM((half_ring, 2, gate_rows, tokens), f32),
            pltpu.VMEM((half_ring, 2 * tokens, width), bf16),
            pltpu.VMEM((2 * tokens, width), bf16),
            pltpu.VMEM((half_ring, 2 * tokens, width), f32),
            pltpu.VMEM((2 * tokens, 2 * ff), bf16),
            pltpu.VMEM((half_ring, 2 * tokens, 128), f32),
            pltpu.VMEM(half_states, f32),
            pltpu.VMEM((tokens, width), f32),
            pltpu.VMEM(half_states, bf16),
            pltpu.VMEM(half_states, bf16),
            pltpu.VMEM(half_states, bf16),
            pltpu.VMEM(half_states, bf16),
            pltpu.VMEM(half_states, bf16),
            pltpu.VMEM(half_states, bf16),
            pltpu.VMEM((2, half_ring, tokens, width), bf16),
            pltpu.VMEM((2, half_ring, tokens, width), bf16),
            dma((3,)),
            dma((3,)),
            dma((3,)),
            dma((3,)),
            dma((half_ring, 2)),
            dma((half_ring, 2)),
            dma((SCAN_PARTS,)),
            dma((SCAN_PARTS,)),
            dma((SCAN_PARTS,)),
            dma((SCAN_PARTS,)),
            dma((SCAN_PARTS,)),
            dma((SCAN_PARTS,)),
            dma((2, half_ring, ROW_PARTS)),
            dma((2, half_ring, ROW_PARTS)),
            dma((2, half_ring, 2)),
            dma((2, half_ring, 2)),
        ],
        compiler_params=pltpu.CompilerParams(
            collective_id=0, has_side_effects=True, vmem_limit_bytes=VMEM_BYTES
        ),
        cost_estimate=pl.CostEstimate(
            flops=12 * count * tokens * width * ff,
            bytes_accessed=6 * width * ff + 10 * tokens * width,
            transcendentals=2 * count * tokens * ff,
        ),
    )(
        queries[0],
        key_rows[0],
        value_rows[0],
        head_gain.reshape(1, width),
        ffn_gain.reshape(1, width),
        expert_ids[0].T,
        router_weight[0].T,
        w_gate,
        w_up,
        w_down,
    )
    layer_out = attention + mixture
    return attention.astype(bf16)[None], layer_out.astype(bf16)[None]


def fits_in_vmem(mesh, arrays):
    count = mesh.shape["seq"]
    queries, w_gate = arrays[0], arrays[7]
    tokens, width = queries.shape[1] // count, queries.shape[2]
    held = count * tokens * width * (2 + 4 + 2 + 2) + 12 * width * w_gate.shape[2]
    return held < VMEM_BYTES * 3 // 4


def solution(mesh):
    def layer(*arrays):
        if fits_in_vmem(mesh, arrays):
            body = functools.partial(per_device_ring, arrays[7].shape[0])
        else:
            body = per_device_routed
        return mapped(body)(*arrays)

    def mapped(body):
        return jax.shard_map(
            body,
            mesh=mesh,
            in_specs=(
                P(("groups", "expert"), "seq", None),
                P(("groups", "expert"), "seq", None),
                P(("groups", "expert"), "seq", None),
                P(),
                P(),
                P(("groups", "expert"), "seq", None),
                P(("groups", "expert"), "seq", None),
                P(("seq", "expert"), None, None),
                P(("seq", "expert"), None, None),
                P(("seq", "expert"), None, None),
            ),
            out_specs=(P(("groups", "expert"), "seq", None), P(("groups", "expert"), "seq", None)),
            check_vma=False,
        )

    return layer
```

```python
import functools

import jax
import jax.numpy as jnp
from jax import lax
from jax.experimental import pallas as pl
from jax.experimental.pallas import tpu as pltpu
from jax.sharding import PartitionSpec as P

HEADS = 16
HEAD_DIM = 128


highest = lax.Precision.HIGHEST
epsilon = 1e-06


def prefix(value, axis, join, neutral):
    count, mine = (lax.axis_size(axis), lax.axis_index(axis))
    pieces = lax.all_gather(value, axis)
    subtotal = jnp.full_like(value, 0) + jnp.asarray(neutral, value.dtype)

    def turn(position, subtotal):
        longer = join(subtotal, pieces[position])
        return jnp.where(position < mine, longer, subtotal)

    return lax.fori_loop(0, count - 1, turn, subtotal)


def add_states(earlier, later):
    return earlier + later


def run_expert(inputs, gate_weight, up_weight, down_weight):
    gate_part = jnp.dot(inputs, gate_weight, preferred_element_type=jnp.float32)
    up_part = jnp.dot(inputs, up_weight, preferred_element_type=jnp.float32)
    expert_hidden = (jax.nn.silu(gate_part) * up_part).astype(jnp.bfloat16)
    return jnp.dot(expert_hidden, down_weight, preferred_element_type=jnp.float32).astype(
        jnp.bfloat16
    )


def to_owners(send_slots):
    return lax.all_to_all(send_slots, ("seq", "expert"), split_axis=0, concat_axis=0, tiled=True)


def from_owners(result_slots):
    return lax.all_to_all(result_slots, ("seq", "expert"), split_axis=0, concat_axis=0, tiled=True)


def per_device_routed(
    queries,
    key_rows,
    value_rows,
    head_gain,
    ffn_gain,
    expert_ids,
    router_weight,
    w_gate,
    w_up,
    w_down,
):
    row_count = queries.shape[1]
    model_width = queries.shape[2]
    block_rows = min(row_count, 512)
    block_count = row_count // block_rows
    block_shape = (block_count, block_rows, HEADS, HEAD_DIM)
    query_blocks = queries.reshape(block_shape)
    key_blocks = key_rows.reshape(block_shape)
    value_blocks = value_rows.reshape(block_shape)
    block_states = jnp.einsum(
        "nthd,nthe->nhde", key_blocks, value_blocks, preferred_element_type=jnp.float32
    )
    local_state = jnp.sum(block_states, axis=0)
    carried = prefix(local_state, "seq", add_states, jnp.zeros_like(local_state))
    starts = carried[None] + jnp.cumsum(block_states, axis=0) - block_states
    causal = jnp.arange(block_rows)[:, None] >= jnp.arange(block_rows)[None, :]
    scores = jnp.einsum(
        "nthd,nuhd->nhtu", query_blocks, key_blocks, preferred_element_type=jnp.float32
    )
    scores = jnp.where(causal, scores, 0.0)
    within = jnp.einsum(
        "nhtu,nuhe->nthe", scores, value_blocks.astype(jnp.float32), precision=highest
    )
    before = jnp.einsum(
        "nthd,nhde->nthe", query_blocks.astype(jnp.float32), starts, precision=highest
    )
    heads_raw = (within + before).reshape(row_count, HEADS, HEAD_DIM)
    mean_square = jnp.mean(heads_raw * heads_raw, axis=-1, keepdims=True)
    attention = (
        (heads_raw * lax.rsqrt(mean_square + epsilon)).reshape(row_count, model_width) * head_gain
    ).astype(jnp.bfloat16)
    attn_float = attention.astype(jnp.float32)
    feature_sq = jnp.mean(attn_float * attn_float, axis=-1, keepdims=True)
    normed = (attn_float * lax.rsqrt(feature_sq + epsilon) * ffn_gain).astype(jnp.bfloat16)
    top_count = expert_ids.shape[2]
    owners = lax.axis_size("seq") * lax.axis_size("expert")
    capacity = min(row_count, 3 * row_count * top_count // (2 * owners))
    slot_total = owners * capacity
    route_flat = expert_ids.reshape(row_count * top_count)
    onehot = (route_flat[:, None] == jnp.arange(owners, dtype=jnp.int32)[None, :]).astype(jnp.int32)
    position = jnp.sum(jnp.cumsum(onehot, axis=0) * onehot, axis=1) - 1
    destination = route_flat * capacity + position
    token_order = jnp.arange(row_count * top_count, dtype=jnp.int32) // top_count
    slot_token = jnp.full((slot_total,), row_count, jnp.int32).at[destination].set(token_order)
    send_slots = jnp.take(normed, slot_token, axis=0, mode="fill", fill_value=0).reshape(
        owners, capacity, model_width
    )
    received = to_owners(send_slots).reshape(slot_total, model_width)
    computed = run_expert(received, w_gate[0], w_up[0], w_down[0])
    returned = from_owners(computed.reshape(owners, capacity, model_width)).reshape(
        slot_total, model_width
    )
    picked = jnp.take(returned, destination, axis=0).reshape(row_count, top_count, model_width)
    shares = router_weight[0] / jnp.sum(router_weight[0], axis=-1, keepdims=True)
    mixture = jnp.einsum("tk,tkd->td", shares, picked.astype(jnp.float32), precision=highest)
    layer_out = (attn_float + mixture).astype(jnp.bfloat16)
    return (
        attention.reshape(1, row_count, model_width),
        layer_out.reshape(1, row_count, model_width),
    )


MESH = pl.DeviceIdType.MESH
VMEM_BYTES = 58 * 1024 * 1024
SCAN_PARTS = 8
ROW_PARTS = 4


def layer_kernel(
    count,
    q_hbm, k_hbm, v_hbm, head_gain, ffn_gain, ids_ref, score_ref, wg_ref, wu_ref, wd_ref,
    att_ref, mix_ref,
    q_ref, k_ref, v_ref, w_in, w_out, gates, rows, normed, partial, hidden, share, state, within,
    a_out, a_in, c_out, c_in, b_out, b_in, sum_in, sum_out,
    in_sem, w_sem, w_send, w_recv, gate_send, gate_recv, a_send, a_recv, c_send, c_recv, b_send, b_recv,
    row_send, row_recv, sum_send, sum_recv,
):
    half_ring = count // 2
    group = lax.axis_index("groups")
    me = lax.axis_index("seq")
    core = lax.axis_index("expert")
    z, y = me // 2, me % 2
    ring = jnp.where(y == 0, z, count - 1 - z)

    def at_ring(place):
        place = lax.rem(place + 2 * count, count)
        seq = jnp.where(place < half_ring, 2 * place, 2 * (count - 1 - place) + 1)
        return (group, seq, core)

    right, left = at_ring(ring + 1), at_ring(ring - 1)
    sibling = (group, me, 1 - core)
    tokens, width = q_ref.shape
    low = tokens // 2
    ff = wg_ref.shape[2]
    part = HEADS // SCAN_PARTS

    barrier = pltpu.get_barrier_semaphore()
    for d in range(1, count):
        pl.semaphore_signal(barrier, inc=1, device_id=at_ring(ring + d), device_id_type=MESH)
    pl.semaphore_signal(barrier, inc=1, device_id=sibling, device_id_type=MESH)

    in_copies = [
        pltpu.make_async_copy(k_hbm, k_ref, in_sem.at[0]),
        pltpu.make_async_copy(v_hbm, v_ref, in_sem.at[1]),
        pltpu.make_async_copy(q_hbm, q_ref, in_sem.at[2]),
    ]
    for c in in_copies:
        c.start()
    own_copies = [
        pltpu.make_async_copy(wg_ref.at[0], w_in.at[0], w_sem.at[0]),
        pltpu.make_async_copy(wu_ref.at[0], w_in.at[1], w_sem.at[1]),
        pltpu.make_async_copy(wd_ref.at[0], w_out.at[pl.ds(0, ff)], w_sem.at[2]),
    ]
    for c in own_copies:
        c.start()

    def head(h):
        return pl.ds(h * HEAD_DIM, HEAD_DIM)

    half_rows = HEADS * HEAD_DIM // 2
    piece = half_rows // SCAN_PARTS
    mine, other = y * half_rows, (1 - y) * half_rows

    def head_state(base, h):
        cols = pl.ds(pl.multiple_of(base + h * HEAD_DIM, HEAD_DIM), HEAD_DIM)
        return lax.dot_general(
            k_ref[:, cols], v_ref[:, cols], (((0,), (0,)), ((), ())),
            preferred_element_type=jnp.float32,
        )

    for c in in_copies[:2]:
        c.wait()
    for h in range(HEADS // 2):
        a_out[head(h), :] = head_state(other, h).astype(jnp.bfloat16)

    pl.semaphore_wait(barrier, count)

    def remote(src, dst, send, recv, where):
        return pltpu.make_async_remote_copy(
            src_ref=src, dst_ref=dst, send_sem=send, recv_sem=recv,
            device_id=where, device_id_type=MESH,
        )

    across = (group, me + 1 - 2 * y, core)
    above = (group, lax.rem(me + 2, count), core)

    def span(j):
        return pl.ds(j * piece, piece)

    def a_copy(j):
        return remote(a_out.at[span(j)], a_in.at[span(j)], a_send.at[j], a_recv.at[j], across)

    def b_copy(j):
        return remote(b_out.at[span(j)], b_in.at[span(j)], b_send.at[j], b_recv.at[j], across)

    def c_copy(j):
        return remote(c_out.at[span(j)], c_in.at[span(j)], c_send.at[j], c_recv.at[j], above)

    for j in range(SCAN_PARTS):
        a_copy(j).start()
    for h in range(HEADS // 2):
        state[head(h), :] = head_state(mine, h)
    in_copies[2].wait()

    gate_rows = gates.shape[2] - 8
    picks = lax.broadcasted_iota(jnp.int32, (gate_rows, tokens), 0)
    scores = score_ref[...]
    named = scores / jnp.sum(scores, axis=0, keepdims=True)
    ids = ids_ref[...]
    dense = jnp.zeros((gate_rows, tokens), jnp.float32)
    for t in range(ids.shape[0]):
        dense += jnp.where(ids[t : t + 1, :] == picks, named[t : t + 1, :], 0.0)
    gates[0, 0, pl.ds(0, gate_rows), :] = dense

    causal = lax.broadcasted_iota(jnp.int32, (tokens, tokens), 0) >= lax.broadcasted_iota(
        jnp.int32, (tokens, tokens), 1
    )
    for h in range(HEADS):
        pair = lax.dot_general(
            q_ref[:, head(h)], k_ref[:, head(h)], (((1,), (1,)), ((), ())),
            preferred_element_type=jnp.float32,
        )
        pair = jnp.where(causal, pair, 0.0).astype(jnp.bfloat16)
        within[:, head(h)] = jnp.dot(pair, v_ref[:, head(h)], preferred_element_type=jnp.float32)

    weight_copies = [
        remote(wg_ref.at[0], w_in.at[2], w_send.at[0], w_recv.at[0], sibling),
        remote(wu_ref.at[0], w_in.at[3], w_send.at[1], w_recv.at[1], sibling),
        remote(wd_ref.at[0], w_out.at[pl.ds(ff, ff)], w_send.at[2], w_recv.at[2], sibling),
    ]

    part_width = width // ROW_PARTS

    def row_copy(side, step, i, origin):
        place = lax.rem(origin + 2 * count, count)
        first = jnp.where(place < half_ring, 0, ROW_PARTS // 2)
        c = lax.rem(first + i, ROW_PARTS)
        cols = pl.ds(pl.multiple_of(c * part_width, part_width), part_width)
        src = rows.at[step - 1, pl.ds(0 if step == 1 else side * tokens, tokens), cols]
        if step < half_ring:
            dst = rows.at[step, pl.ds(side * tokens, tokens), cols]
        else:
            dst = rows.at[0, pl.ds(tokens, tokens), cols]
        return remote(
            src, dst, row_send.at[side, step - 1, i], row_recv.at[side, step - 1, i],
            right if side == 0 else left,
        )

    def row_out(side, step, i):
        back = step - 1
        return row_copy(side, step, i, ring - back if side == 0 else ring + back)

    def row_arrival(side, step, i):
        return row_copy(side, step, i, ring - step if side == 0 else ring + step)

    def goes(side, step, i):
        return step < half_ring or (i < ROW_PARTS // 2) == (side == 0)

    def chain(j):
        a_copy(j).wait_recv()

        @pl.when(z == 0)
        def _():
            c_in[span(j), :] = jnp.zeros((piece, HEAD_DIM), jnp.bfloat16)

        @pl.when(z > 0)
        def _():
            c_copy(j).wait_recv()

        earlier = c_in[span(j), :].astype(jnp.float32)
        own = state[span(j), :]
        c_out[span(j), :] = (
            earlier + (own + a_in[span(j), :].astype(jnp.float32))
        ).astype(jnp.bfloat16)

        @pl.when(z < half_ring - 1)
        def _():
            c_copy(j).start()

        b_out[span(j), :] = (earlier + jnp.where(y == 0, own, 0.0)).astype(jnp.bfloat16)
        b_copy(j).start()

    heads_each = piece // HEAD_DIM

    def attend(j):
        if j < SCAN_PARTS:
            base, k = mine, j
            start = c_in[span(k), :].astype(jnp.float32) + jnp.where(
                y == 1, a_in[span(k), :].astype(jnp.float32), 0.0
            )
            start = start.astype(jnp.bfloat16)
        else:
            base, k = other, j - SCAN_PARTS
            b_copy(k).wait_recv()
            start = b_in[span(k), :]
        squares = jnp.zeros((tokens, HEAD_DIM), jnp.float32)
        for i in range(heads_each):
            cols = pl.ds(
                pl.multiple_of(base + k * piece + i * HEAD_DIM, HEAD_DIM), HEAD_DIM
            )
            raw = within[:, cols] + jnp.dot(
                q_ref[:, cols], start[i * HEAD_DIM : (i + 1) * HEAD_DIM],
                preferred_element_type=jnp.float32,
            )
            mean_square = jnp.mean(raw * raw, axis=-1, keepdims=True)
            att = (raw * lax.rsqrt(mean_square + epsilon) * head_gain[:, cols]).astype(
                jnp.bfloat16
            )
            rows[0, pl.ds(0, tokens), cols] = att
            att = att.astype(jnp.float32)
            att_ref[:, cols] = att
            squares += att * att
        each = 2 * SCAN_PARTS // ROW_PARTS
        if (j + 1) % each == 0:
            for side in range(2):
                row_out(side, 1, j // each).start()
        return squares

    square = jnp.zeros((tokens, HEAD_DIM), jnp.float32)
    for j in range(SCAN_PARTS):
        chain(j)
        if j % 2 == 1 and j > 2:
            square += attend(j - 3) + attend(j - 2)
    for j in range(SCAN_PARTS - 2, 2 * SCAN_PARTS):
        square += attend(j)
        if j - SCAN_PARTS + 2 < len(weight_copies):
            weight_copies[j - SCAN_PARTS + 2].start()

    scale = lax.rsqrt(jnp.sum(jnp.transpose(square), axis=0, keepdims=True) / width + epsilon)
    gates[0, 0, pl.ds(gate_rows, 8), :] = jnp.broadcast_to(scale, (8, tokens))
    gate_copies = []
    for d in range(1, count):
        slot = (d, 0) if d < half_ring else ((0, 1) if d == half_ring else (count - d, 1))
        gate_copies.append(
            remote(gates.at[0, 0], gates.at[slot[0], slot[1]],
                   gate_send.at[slot[0], slot[1]], gate_recv.at[slot[0], slot[1]],
                   at_ring(ring + d))
        )
    for c in gate_copies:
        c.start()

    def row_span(side, h):
        return pl.ds(side * tokens + h * low, low)

    def expert_pieces(index, first, size):
        here = pl.ds(first, size)

        def norm():
            scale = share[index, here, 2:3]
            for h in range(HEADS):
                normed[here, head(h)] = (
                    rows[index, here, head(h)].astype(jnp.float32) * scale * ffn_gain[:, head(h)]
                ).astype(jnp.bfloat16)

        def into_hidden(e):
            x = normed[here, :]
            gate_part = jnp.dot(x, w_in[2 * e], preferred_element_type=jnp.float32)
            up_part = jnp.dot(x, w_in[2 * e + 1], preferred_element_type=jnp.float32)
            act = gate_part / (1.0 + jnp.exp(-gate_part)) * up_part
            hidden[here, pl.ds(e * ff, ff)] = (
                act * share[index, here, e : e + 1]
            ).astype(jnp.bfloat16)

        def from_hidden():
            partial[index, here, :] = jnp.dot(
                hidden[here, :], w_out[...], preferred_element_type=jnp.float32
            )

        return [
            norm,
            functools.partial(into_hidden, 0),
            functools.partial(into_hidden, 1),
            from_hidden,
        ]

    def sum_copy(side, step, h):
        here = (side, step - 1, pl.ds(h * low, low))
        return remote(
            sum_out.at[here], sum_in.at[here],
            sum_send.at[side, step - 1, h], sum_recv.at[side, step - 1, h],
            right if side == 0 else left,
        )

    def sum_step(side, step, h):
        index = half_ring - step + 1 if step > 1 else 0
        value = partial[index, row_span(1 if step == 1 else 1 - side, h), :]
        if step > 2 or (step == 2 and h == side):
            sum_copy(side, step - 1, h).wait_recv()
            value += sum_in[side, step - 2, pl.ds(h * low, low), :].astype(jnp.float32)
        sum_out[side, step - 1, pl.ds(h * low, low), :] = value.astype(jnp.bfloat16)
        sum_copy(side, step, h).start()

    def take(step, i):
        for side in range(2):
            if goes(side, step, i):
                row_arrival(side, step, i).wait_recv()
            if step < half_ring and goes(side, step + 1, i):
                row_out(side, step + 1, i).start()

    for i in range(ROW_PARTS):
        take(1, i)
    for c in own_copies:
        c.wait()
    for c in weight_copies:
        c.wait_recv()
    for c in gate_copies:
        c.wait_recv()
    line = lax.broadcasted_iota(jnp.int32, (gate_rows + 8, 128), 0)
    lane = lax.broadcasted_iota(jnp.int32, (gate_rows + 8, 128), 1)
    wanted = jnp.where(lane == 0, 2 * me + core, jnp.where(lane == 1, 2 * me + 1 - core, gate_rows))
    chosen = ((line == wanted) & (lane < 3)).astype(jnp.float32)
    for index in range(half_ring):
        for side in range(2):
            share[index, pl.ds(side * tokens, tokens), :] = lax.dot_general(
                gates[index, side], chosen, (((0,), (0,)), ((), ())),
                preferred_element_type=jnp.float32, precision=highest,
            )
    for step in range(1, half_ring):
        for i, work in enumerate(expert_pieces(step, 0, 2 * tokens)):
            if step + 1 < half_ring:
                take(step + 1, i)
            work()
    for side in range(2):
        sum_step(side, 2, 1 - side)
    for i in range(ROW_PARTS):
        take(half_ring, i)
    for work in expert_pieces(0, tokens, tokens):
        work()
    for side in range(2):
        sum_step(side, 1, side)
    later = [(step, first) for step in range(2, half_ring + 1) for first in range(2)][1:]
    own_work = expert_pieces(0, 0, tokens)
    for step, first in later:
        for side in range(2):
            sum_step(side, step, (1 - side + first) % 2)
        if own_work:
            own_work.pop(0)()
    for work in own_work:
        work()
    for h in range(2):
        total = partial[0, row_span(0, h), :]
        for side in range(2):
            sum_copy(side, half_ring, h).wait_recv()
            total += sum_in[side, half_ring - 1, pl.ds(h * low, low), :].astype(jnp.float32)
        mix_ref[pl.ds(h * low, low), :] = total

    for c in weight_copies + gate_copies:
        c.wait_send()
    for j in range(SCAN_PARTS):
        @pl.when(z < half_ring - 1)
        def _():
            c_copy(j).wait_send()

        a_copy(j).wait_send()
        b_copy(j).wait_send()
    for side in range(2):
        for step in range(1, half_ring + 1):
            for i in range(ROW_PARTS):
                if goes(side, step, i):
                    row_out(side, step, i).wait_send()
            for h in range(2):
                if step > 1 or h == side:
                    sum_copy(side, step, h).wait_send()


def per_device_ring(
    experts,
    queries,
    key_rows,
    value_rows,
    head_gain,
    ffn_gain,
    expert_ids,
    router_weight,
    w_gate,
    w_up,
    w_down,
):
    count = lax.axis_size("seq")
    half_ring = count // 2
    tokens, width = queries.shape[1:]
    ff = w_gate.shape[2]
    bf16, f32 = jnp.bfloat16, jnp.float32
    vmem = pl.BlockSpec(memory_space=pltpu.VMEM)
    hbm = pl.BlockSpec(memory_space=pl.ANY)
    dma = pltpu.SemaphoreType.DMA
    half_states = (HEADS * HEAD_DIM // 2, HEAD_DIM)
    gate_rows = -(-experts // 8) * 8 + 8
    attention, mixture = pl.pallas_call(
        functools.partial(layer_kernel, count),
        out_shape=[jax.ShapeDtypeStruct((tokens, width), f32)] * 2,
        in_specs=[hbm] * 3 + [vmem] * 4 + [hbm] * 3,
        out_specs=[vmem] * 2,
        scratch_shapes=[
            pltpu.VMEM((tokens, width), bf16),
            pltpu.VMEM((tokens, width), bf16),
            pltpu.VMEM((tokens, width), bf16),
            pltpu.VMEM((4, width, ff), bf16),
            pltpu.VMEM((2 * ff, width), bf16),
            pltpu.VMEM((half_ring, 2, gate_rows, tokens), f32),
            pltpu.VMEM((half_ring, 2 * tokens, width), bf16),
            pltpu.VMEM((2 * tokens, width), bf16),
            pltpu.VMEM((half_ring, 2 * tokens, width), f32),
            pltpu.VMEM((2 * tokens, 2 * ff), bf16),
            pltpu.VMEM((half_ring, 2 * tokens, 128), f32),
            pltpu.VMEM(half_states, f32),
            pltpu.VMEM((tokens, width), f32),
            pltpu.VMEM(half_states, bf16),
            pltpu.VMEM(half_states, bf16),
            pltpu.VMEM(half_states, bf16),
            pltpu.VMEM(half_states, bf16),
            pltpu.VMEM(half_states, bf16),
            pltpu.VMEM(half_states, bf16),
            pltpu.VMEM((2, half_ring, tokens, width), bf16),
            pltpu.VMEM((2, half_ring, tokens, width), bf16),
            dma((3,)),
            dma((3,)),
            dma((3,)),
            dma((3,)),
            dma((half_ring, 2)),
            dma((half_ring, 2)),
            dma((SCAN_PARTS,)),
            dma((SCAN_PARTS,)),
            dma((SCAN_PARTS,)),
            dma((SCAN_PARTS,)),
            dma((SCAN_PARTS,)),
            dma((SCAN_PARTS,)),
            dma((2, half_ring, ROW_PARTS)),
            dma((2, half_ring, ROW_PARTS)),
            dma((2, half_ring, 2)),
            dma((2, half_ring, 2)),
        ],
        compiler_params=pltpu.CompilerParams(
            collective_id=0, has_side_effects=True, vmem_limit_bytes=VMEM_BYTES
        ),
        cost_estimate=pl.CostEstimate(
            flops=12 * count * tokens * width * ff,
            bytes_accessed=6 * width * ff + 10 * tokens * width,
            transcendentals=2 * count * tokens * ff,
        ),
    )(
        queries[0],
        key_rows[0],
        value_rows[0],
        head_gain.reshape(1, width),
        ffn_gain.reshape(1, width),
        expert_ids[0].T,
        router_weight[0].T,
        w_gate,
        w_up,
        w_down,
    )
    layer_out = attention + mixture
    return attention.astype(bf16)[None], layer_out.astype(bf16)[None]


def fits_in_vmem(mesh, arrays):
    count = mesh.shape["seq"]
    queries, w_gate = arrays[0], arrays[7]
    tokens, width = queries.shape[1] // count, queries.shape[2]
    held = count * tokens * width * (2 + 4 + 2 + 2) + 12 * width * w_gate.shape[2]
    return held < VMEM_BYTES * 3 // 4


def solution(mesh):
    def layer(*arrays):
        if fits_in_vmem(mesh, arrays):
            body = functools.partial(per_device_ring, arrays[7].shape[0])
        else:
            body = per_device_routed
        return mapped(body)(*arrays)

    def mapped(body):
        return jax.shard_map(
            body,
            mesh=mesh,
            in_specs=(
                P(("groups", "expert"), "seq", None),
                P(("groups", "expert"), "seq", None),
                P(("groups", "expert"), "seq", None),
                P(),
                P(),
                P(("groups", "expert"), "seq", None),
                P(("groups", "expert"), "seq", None),
                P(("seq", "expert"), None, None),
                P(("seq", "expert"), None, None),
                P(("seq", "expert"), None, None),
            ),
            out_specs=(P(("groups", "expert"), "seq", None), P(("groups", "expert"), "seq", None)),
            check_vma=False,
        )

    return layer
```

```python
import functools

import jax
import jax.numpy as jnp
from jax import lax
from jax.experimental import pallas as pl
from jax.experimental.pallas import tpu as pltpu
from jax.sharding import PartitionSpec as P

HEADS = 16
HEAD_DIM = 128


highest = lax.Precision.HIGHEST
epsilon = 1e-06


def prefix(value, axis, join, neutral):
    count, mine = (lax.axis_size(axis), lax.axis_index(axis))
    pieces = lax.all_gather(value, axis)
    subtotal = jnp.full_like(value, 0) + jnp.asarray(neutral, value.dtype)

    def turn(position, subtotal):
        longer = join(subtotal, pieces[position])
        return jnp.where(position < mine, longer, subtotal)

    return lax.fori_loop(0, count - 1, turn, subtotal)


def add_states(earlier, later):
    return earlier + later


def run_expert(inputs, gate_weight, up_weight, down_weight):
    gate_part = jnp.dot(inputs, gate_weight, preferred_element_type=jnp.float32)
    up_part = jnp.dot(inputs, up_weight, preferred_element_type=jnp.float32)
    expert_hidden = (jax.nn.silu(gate_part) * up_part).astype(jnp.bfloat16)
    return jnp.dot(expert_hidden, down_weight, preferred_element_type=jnp.float32).astype(
        jnp.bfloat16
    )


def to_owners(send_slots):
    return lax.all_to_all(send_slots, ("seq", "expert"), split_axis=0, concat_axis=0, tiled=True)


def from_owners(result_slots):
    return lax.all_to_all(result_slots, ("seq", "expert"), split_axis=0, concat_axis=0, tiled=True)


def per_device_routed(
    queries,
    key_rows,
    value_rows,
    head_gain,
    ffn_gain,
    expert_ids,
    router_weight,
    w_gate,
    w_up,
    w_down,
):
    row_count = queries.shape[1]
    model_width = queries.shape[2]
    block_rows = min(row_count, 512)
    block_count = row_count // block_rows
    block_shape = (block_count, block_rows, HEADS, HEAD_DIM)
    query_blocks = queries.reshape(block_shape)
    key_blocks = key_rows.reshape(block_shape)
    value_blocks = value_rows.reshape(block_shape)
    block_states = jnp.einsum(
        "nthd,nthe->nhde", key_blocks, value_blocks, preferred_element_type=jnp.float32
    )
    local_state = jnp.sum(block_states, axis=0)
    carried = prefix(local_state, "seq", add_states, jnp.zeros_like(local_state))
    starts = carried[None] + jnp.cumsum(block_states, axis=0) - block_states
    causal = jnp.arange(block_rows)[:, None] >= jnp.arange(block_rows)[None, :]
    scores = jnp.einsum(
        "nthd,nuhd->nhtu", query_blocks, key_blocks, preferred_element_type=jnp.float32
    )
    scores = jnp.where(causal, scores, 0.0)
    within = jnp.einsum(
        "nhtu,nuhe->nthe", scores, value_blocks.astype(jnp.float32), precision=highest
    )
    before = jnp.einsum(
        "nthd,nhde->nthe", query_blocks.astype(jnp.float32), starts, precision=highest
    )
    heads_raw = (within + before).reshape(row_count, HEADS, HEAD_DIM)
    mean_square = jnp.mean(heads_raw * heads_raw, axis=-1, keepdims=True)
    attention = (
        (heads_raw * lax.rsqrt(mean_square + epsilon)).reshape(row_count, model_width) * head_gain
    ).astype(jnp.bfloat16)
    attn_float = attention.astype(jnp.float32)
    feature_sq = jnp.mean(attn_float * attn_float, axis=-1, keepdims=True)
    normed = (attn_float * lax.rsqrt(feature_sq + epsilon) * ffn_gain).astype(jnp.bfloat16)
    top_count = expert_ids.shape[2]
    owners = lax.axis_size("seq") * lax.axis_size("expert")
    capacity = min(row_count, 3 * row_count * top_count // (2 * owners))
    slot_total = owners * capacity
    route_flat = expert_ids.reshape(row_count * top_count)
    onehot = (route_flat[:, None] == jnp.arange(owners, dtype=jnp.int32)[None, :]).astype(jnp.int32)
    position = jnp.sum(jnp.cumsum(onehot, axis=0) * onehot, axis=1) - 1
    destination = route_flat * capacity + position
    token_order = jnp.arange(row_count * top_count, dtype=jnp.int32) // top_count
    slot_token = jnp.full((slot_total,), row_count, jnp.int32).at[destination].set(token_order)
    send_slots = jnp.take(normed, slot_token, axis=0, mode="fill", fill_value=0).reshape(
        owners, capacity, model_width
    )
    received = to_owners(send_slots).reshape(slot_total, model_width)
    computed = run_expert(received, w_gate[0], w_up[0], w_down[0])
    returned = from_owners(computed.reshape(owners, capacity, model_width)).reshape(
        slot_total, model_width
    )
    picked = jnp.take(returned, destination, axis=0).reshape(row_count, top_count, model_width)
    shares = router_weight[0] / jnp.sum(router_weight[0], axis=-1, keepdims=True)
    mixture = jnp.einsum("tk,tkd->td", shares, picked.astype(jnp.float32), precision=highest)
    layer_out = (attn_float + mixture).astype(jnp.bfloat16)
    return (
        attention.reshape(1, row_count, model_width),
        layer_out.reshape(1, row_count, model_width),
    )


MESH = pl.DeviceIdType.MESH
VMEM_BYTES = 58 * 1024 * 1024
SCAN_PARTS = 8
ROW_PARTS = 4


def layer_kernel(
    count,
    q_hbm, k_hbm, v_hbm, head_gain, ffn_gain, ids_ref, score_ref, wg_ref, wu_ref, wd_ref,
    att_ref, mix_ref,
    q_ref, k_ref, v_ref, w_in, w_out, gates, rows, normed, partial, hidden, share, state, within,
    a_out, a_in, c_out, c_in, b_out, b_in, sum_in, sum_out,
    in_sem, w_sem, w_send, w_recv, gate_send, gate_recv, a_send, a_recv, c_send, c_recv, b_send, b_recv,
    row_send, row_recv, sum_send, sum_recv,
):
    half_ring = count // 2
    group = lax.axis_index("groups")
    me = lax.axis_index("seq")
    core = lax.axis_index("expert")
    z, y = me // 2, me % 2
    ring = jnp.where(y == 0, z, count - 1 - z)

    def at_ring(place):
        place = lax.rem(place + 2 * count, count)
        seq = jnp.where(place < half_ring, 2 * place, 2 * (count - 1 - place) + 1)
        return (group, seq, core)

    right, left = at_ring(ring + 1), at_ring(ring - 1)
    sibling = (group, me, 1 - core)
    tokens, width = q_ref.shape
    low = tokens // 2
    ff = wg_ref.shape[2]
    part = HEADS // SCAN_PARTS

    barrier = pltpu.get_barrier_semaphore()
    for d in range(1, count):
        pl.semaphore_signal(barrier, inc=1, device_id=at_ring(ring + d), device_id_type=MESH)
    pl.semaphore_signal(barrier, inc=1, device_id=sibling, device_id_type=MESH)

    in_copies = [
        pltpu.make_async_copy(k_hbm, k_ref, in_sem.at[0]),
        pltpu.make_async_copy(v_hbm, v_ref, in_sem.at[1]),
        pltpu.make_async_copy(q_hbm, q_ref, in_sem.at[2]),
    ]
    for c in in_copies:
        c.start()
    own_copies = [
        pltpu.make_async_copy(wg_ref.at[0], w_in.at[0], w_sem.at[0]),
        pltpu.make_async_copy(wu_ref.at[0], w_in.at[1], w_sem.at[1]),
        pltpu.make_async_copy(wd_ref.at[0], w_out.at[pl.ds(0, ff)], w_sem.at[2]),
    ]
    for c in own_copies:
        c.start()

    def head(h):
        return pl.ds(h * HEAD_DIM, HEAD_DIM)

    half_rows = HEADS * HEAD_DIM // 2
    piece = half_rows // SCAN_PARTS
    mine, other = y * half_rows, (1 - y) * half_rows

    def head_state(base, h):
        cols = pl.ds(pl.multiple_of(base + h * HEAD_DIM, HEAD_DIM), HEAD_DIM)
        return lax.dot_general(
            k_ref[:, cols], v_ref[:, cols], (((0,), (0,)), ((), ())),
            preferred_element_type=jnp.float32,
        )

    for c in in_copies[:2]:
        c.wait()
    for h in range(HEADS // 2):
        a_out[head(h), :] = head_state(other, h).astype(jnp.bfloat16)

    pl.semaphore_wait(barrier, count)

    def remote(src, dst, send, recv, where):
        return pltpu.make_async_remote_copy(
            src_ref=src, dst_ref=dst, send_sem=send, recv_sem=recv,
            device_id=where, device_id_type=MESH,
        )

    across = (group, me + 1 - 2 * y, core)
    above = (group, lax.rem(me + 2, count), core)

    def span(j):
        return pl.ds(j * piece, piece)

    def a_copy(j):
        return remote(a_out.at[span(j)], a_in.at[span(j)], a_send.at[j], a_recv.at[j], across)

    def b_copy(j):
        return remote(b_out.at[span(j)], b_in.at[span(j)], b_send.at[j], b_recv.at[j], across)

    def c_copy(j):
        return remote(c_out.at[span(j)], c_in.at[span(j)], c_send.at[j], c_recv.at[j], above)

    for j in range(SCAN_PARTS):
        a_copy(j).start()
    for h in range(HEADS // 2):
        state[head(h), :] = head_state(mine, h)
    in_copies[2].wait()

    gate_rows = gates.shape[2] - 8
    picks = lax.broadcasted_iota(jnp.int32, (gate_rows, tokens), 0)
    scores = score_ref[...]
    named = scores / jnp.sum(scores, axis=0, keepdims=True)
    ids = ids_ref[...]
    dense = jnp.zeros((gate_rows, tokens), jnp.float32)
    for t in range(ids.shape[0]):
        dense += jnp.where(ids[t : t + 1, :] == picks, named[t : t + 1, :], 0.0)
    gates[0, 0, pl.ds(0, gate_rows), :] = dense

    causal = lax.broadcasted_iota(jnp.int32, (tokens, tokens), 0) >= lax.broadcasted_iota(
        jnp.int32, (tokens, tokens), 1
    )
    for h in range(HEADS):
        pair = lax.dot_general(
            q_ref[:, head(h)], k_ref[:, head(h)], (((1,), (1,)), ((), ())),
            preferred_element_type=jnp.float32,
        )
        pair = jnp.where(causal, pair, 0.0).astype(jnp.bfloat16)
        within[:, head(h)] = jnp.dot(pair, v_ref[:, head(h)], preferred_element_type=jnp.float32)

    weight_copies = [
        remote(wg_ref.at[0], w_in.at[2], w_send.at[0], w_recv.at[0], sibling),
        remote(wu_ref.at[0], w_in.at[3], w_send.at[1], w_recv.at[1], sibling),
        remote(wd_ref.at[0], w_out.at[pl.ds(ff, ff)], w_send.at[2], w_recv.at[2], sibling),
    ]

    part_width = width // ROW_PARTS

    def row_copy(side, step, i, origin):
        place = lax.rem(origin + 2 * count, count)
        first = jnp.where(place < half_ring, 0, ROW_PARTS // 2)
        c = lax.rem(first + i, ROW_PARTS)
        cols = pl.ds(pl.multiple_of(c * part_width, part_width), part_width)
        src = rows.at[step - 1, pl.ds(0 if step == 1 else side * tokens, tokens), cols]
        if step < half_ring:
            dst = rows.at[step, pl.ds(side * tokens, tokens), cols]
        else:
            dst = rows.at[0, pl.ds(tokens, tokens), cols]
        return remote(
            src, dst, row_send.at[side, step - 1, i], row_recv.at[side, step - 1, i],
            right if side == 0 else left,
        )

    def row_out(side, step, i):
        back = step - 1
        return row_copy(side, step, i, ring - back if side == 0 else ring + back)

    def row_arrival(side, step, i):
        return row_copy(side, step, i, ring - step if side == 0 else ring + step)

    def goes(side, step, i):
        return step < half_ring or (i < ROW_PARTS // 2) == (side == 0)

    def chain(j):
        a_copy(j).wait_recv()

        @pl.when(z == 0)
        def _():
            c_in[span(j), :] = jnp.zeros((piece, HEAD_DIM), jnp.bfloat16)

        @pl.when(z > 0)
        def _():
            c_copy(j).wait_recv()

        earlier = c_in[span(j), :].astype(jnp.float32)
        own = state[span(j), :]
        c_out[span(j), :] = (
            earlier + (own + a_in[span(j), :].astype(jnp.float32))
        ).astype(jnp.bfloat16)

        @pl.when(z < half_ring - 1)
        def _():
            c_copy(j).start()

        b_out[span(j), :] = (earlier + jnp.where(y == 0, own, 0.0)).astype(jnp.bfloat16)
        b_copy(j).start()

    heads_each = piece // HEAD_DIM

    def attend(j):
        if j < SCAN_PARTS:
            base, k = mine, j
            start = c_in[span(k), :].astype(jnp.float32) + jnp.where(
                y == 1, a_in[span(k), :].astype(jnp.float32), 0.0
            )
            start = start.astype(jnp.bfloat16)
        else:
            base, k = other, j - SCAN_PARTS
            b_copy(k).wait_recv()
            start = b_in[span(k), :]
        squares = jnp.zeros((tokens, HEAD_DIM), jnp.float32)
        for i in range(heads_each):
            cols = pl.ds(
                pl.multiple_of(base + k * piece + i * HEAD_DIM, HEAD_DIM), HEAD_DIM
            )
            raw = within[:, cols] + jnp.dot(
                q_ref[:, cols], start[i * HEAD_DIM : (i + 1) * HEAD_DIM],
                preferred_element_type=jnp.float32,
            )
            mean_square = jnp.mean(raw * raw, axis=-1, keepdims=True)
            att = (raw * lax.rsqrt(mean_square + epsilon) * head_gain[:, cols]).astype(
                jnp.bfloat16
            )
            rows[0, pl.ds(0, tokens), cols] = att
            att = att.astype(jnp.float32)
            att_ref[:, cols] = att
            squares += att * att
        each = 2 * SCAN_PARTS // ROW_PARTS
        if (j + 1) % each == 0:
            for side in range(2):
                row_out(side, 1, j // each).start()
        return squares

    square = jnp.zeros((tokens, HEAD_DIM), jnp.float32)
    for j in range(SCAN_PARTS):
        chain(j)
        if j % 2 == 1 and j > 2:
            square += attend(j - 3) + attend(j - 2)
    for j in range(SCAN_PARTS - 2, 2 * SCAN_PARTS):
        square += attend(j)
        if j - SCAN_PARTS + 2 < len(weight_copies):
            weight_copies[j - SCAN_PARTS + 2].start()

    scale = lax.rsqrt(jnp.sum(jnp.transpose(square), axis=0, keepdims=True) / width + epsilon)
    gates[0, 0, pl.ds(gate_rows, 8), :] = jnp.broadcast_to(scale, (8, tokens))
    gate_copies = {}
    for d in range(1, count):
        slot = (d, 0) if d < half_ring else ((0, 1) if d == half_ring else (count - d, 1))
        gate_copies[slot] = remote(
            gates.at[0, 0], gates.at[slot[0], slot[1]],
            gate_send.at[slot[0], slot[1]], gate_recv.at[slot[0], slot[1]],
            at_ring(ring + d),
        )
        gate_copies[slot].start()

    def row_span(side, h):
        return pl.ds(side * tokens + h * low, low)

    line = lax.broadcasted_iota(jnp.int32, (gate_rows + 8, 128), 0)
    lane = lax.broadcasted_iota(jnp.int32, (gate_rows + 8, 128), 1)
    wanted = jnp.where(lane == 0, 2 * me + core, jnp.where(lane == 1, 2 * me + 1 - core, gate_rows))
    chosen = ((line == wanted) & (lane < 3)).astype(jnp.float32)

    def expert_pieces(index, first, size):
        here = pl.ds(first, size)

        def norm():
            for side in range(first // tokens, (first + size) // tokens):
                if (index, side) != (0, 0):
                    gate_copies[(index, side)].wait_recv()
                share[index, pl.ds(side * tokens, tokens), :] = lax.dot_general(
                    gates[index, side], chosen, (((0,), (0,)), ((), ())),
                    preferred_element_type=jnp.float32, precision=highest,
                )
            scale = share[index, here, 2:3]
            for h in range(HEADS):
                normed[here, head(h)] = (
                    rows[index, here, head(h)].astype(jnp.float32) * scale * ffn_gain[:, head(h)]
                ).astype(jnp.bfloat16)

        def into_hidden(e):
            x = normed[here, :]
            gate_part = jnp.dot(x, w_in[2 * e], preferred_element_type=jnp.float32)
            up_part = jnp.dot(x, w_in[2 * e + 1], preferred_element_type=jnp.float32)
            act = gate_part / (1.0 + jnp.exp(-gate_part)) * up_part
            hidden[here, pl.ds(e * ff, ff)] = (
                act * share[index, here, e : e + 1]
            ).astype(jnp.bfloat16)

        def from_hidden():
            partial[index, here, :] = jnp.dot(
                hidden[here, :], w_out[...], preferred_element_type=jnp.float32
            )

        return [
            norm,
            functools.partial(into_hidden, 0),
            functools.partial(into_hidden, 1),
            from_hidden,
        ]

    def sum_copy(side, step, h):
        here = (side, step - 1, pl.ds(h * low, low))
        return remote(
            sum_out.at[here], sum_in.at[here],
            sum_send.at[side, step - 1, h], sum_recv.at[side, step - 1, h],
            right if side == 0 else left,
        )

    def sum_step(side, step, h):
        index = half_ring - step + 1 if step > 1 else 0
        value = partial[index, row_span(1 if step == 1 else 1 - side, h), :]
        if step > 2 or (step == 2 and h == side):
            sum_copy(side, step - 1, h).wait_recv()
            value += sum_in[side, step - 2, pl.ds(h * low, low), :].astype(jnp.float32)
        sum_out[side, step - 1, pl.ds(h * low, low), :] = value.astype(jnp.bfloat16)
        sum_copy(side, step, h).start()

    def take(step, i):
        for side in range(2):
            if goes(side, step, i):
                row_arrival(side, step, i).wait_recv()
            if step < half_ring and goes(side, step + 1, i):
                row_out(side, step + 1, i).start()

    def arrive(i):
        if i == 1:
            own_copies[0].wait()
            own_copies[1].wait()
        if i == 2:
            weight_copies[0].wait_recv()
            weight_copies[1].wait_recv()
        if i == 3:
            own_copies[2].wait()
            weight_copies[2].wait_recv()

    for i in range(ROW_PARTS):
        take(1, i)
    for step in range(1, half_ring):
        for i, work in enumerate(expert_pieces(step, 0, 2 * tokens)):
            if step == 1:
                arrive(i)
            work()
            if step + 1 < half_ring:
                take(step + 1, i)
    for side in range(2):
        sum_step(side, 2, 1 - side)
    for i in range(ROW_PARTS):
        take(half_ring, i)
    for work in expert_pieces(0, tokens, tokens):
        work()
    for side in range(2):
        sum_step(side, 1, side)
    later = [(step, first) for step in range(2, half_ring + 1) for first in range(2)][1:]
    own_work = expert_pieces(0, 0, tokens)
    for step, first in later:
        for side in range(2):
            sum_step(side, step, (1 - side + first) % 2)
        if own_work:
            own_work.pop(0)()
    for work in own_work:
        work()
    for h in range(2):
        total = partial[0, row_span(0, h), :]
        for side in range(2):
            sum_copy(side, half_ring, h).wait_recv()
            total += sum_in[side, half_ring - 1, pl.ds(h * low, low), :].astype(jnp.float32)
        mix_ref[pl.ds(h * low, low), :] = total

    for c in weight_copies + list(gate_copies.values()):
        c.wait_send()
    for j in range(SCAN_PARTS):
        @pl.when(z < half_ring - 1)
        def _():
            c_copy(j).wait_send()

        a_copy(j).wait_send()
        b_copy(j).wait_send()
    for side in range(2):
        for step in range(1, half_ring + 1):
            for i in range(ROW_PARTS):
                if goes(side, step, i):
                    row_out(side, step, i).wait_send()
            for h in range(2):
                if step > 1 or h == side:
                    sum_copy(side, step, h).wait_send()


def per_device_ring(
    experts,
    queries,
    key_rows,
    value_rows,
    head_gain,
    ffn_gain,
    expert_ids,
    router_weight,
    w_gate,
    w_up,
    w_down,
):
    count = lax.axis_size("seq")
    half_ring = count // 2
    tokens, width = queries.shape[1:]
    ff = w_gate.shape[2]
    bf16, f32 = jnp.bfloat16, jnp.float32
    vmem = pl.BlockSpec(memory_space=pltpu.VMEM)
    hbm = pl.BlockSpec(memory_space=pl.ANY)
    dma = pltpu.SemaphoreType.DMA
    half_states = (HEADS * HEAD_DIM // 2, HEAD_DIM)
    gate_rows = -(-experts // 8) * 8 + 8
    attention, mixture = pl.pallas_call(
        functools.partial(layer_kernel, count),
        out_shape=[jax.ShapeDtypeStruct((tokens, width), f32)] * 2,
        in_specs=[hbm] * 3 + [vmem] * 4 + [hbm] * 3,
        out_specs=[vmem] * 2,
        scratch_shapes=[
            pltpu.VMEM((tokens, width), bf16),
            pltpu.VMEM((tokens, width), bf16),
            pltpu.VMEM((tokens, width), bf16),
            pltpu.VMEM((4, width, ff), bf16),
            pltpu.VMEM((2 * ff, width), bf16),
            pltpu.VMEM((half_ring, 2, gate_rows, tokens), f32),
            pltpu.VMEM((half_ring, 2 * tokens, width), bf16),
            pltpu.VMEM((2 * tokens, width), bf16),
            pltpu.VMEM((half_ring, 2 * tokens, width), f32),
            pltpu.VMEM((2 * tokens, 2 * ff), bf16),
            pltpu.VMEM((half_ring, 2 * tokens, 128), f32),
            pltpu.VMEM(half_states, f32),
            pltpu.VMEM((tokens, width), f32),
            pltpu.VMEM(half_states, bf16),
            pltpu.VMEM(half_states, bf16),
            pltpu.VMEM(half_states, bf16),
            pltpu.VMEM(half_states, bf16),
            pltpu.VMEM(half_states, bf16),
            pltpu.VMEM(half_states, bf16),
            pltpu.VMEM((2, half_ring, tokens, width), bf16),
            pltpu.VMEM((2, half_ring, tokens, width), bf16),
            dma((3,)),
            dma((3,)),
            dma((3,)),
            dma((3,)),
            dma((half_ring, 2)),
            dma((half_ring, 2)),
            dma((SCAN_PARTS,)),
            dma((SCAN_PARTS,)),
            dma((SCAN_PARTS,)),
            dma((SCAN_PARTS,)),
            dma((SCAN_PARTS,)),
            dma((SCAN_PARTS,)),
            dma((2, half_ring, ROW_PARTS)),
            dma((2, half_ring, ROW_PARTS)),
            dma((2, half_ring, 2)),
            dma((2, half_ring, 2)),
        ],
        compiler_params=pltpu.CompilerParams(
            collective_id=0, has_side_effects=True, vmem_limit_bytes=VMEM_BYTES
        ),
        cost_estimate=pl.CostEstimate(
            flops=12 * count * tokens * width * ff,
            bytes_accessed=6 * width * ff + 10 * tokens * width,
            transcendentals=2 * count * tokens * ff,
        ),
    )(
        queries[0],
        key_rows[0],
        value_rows[0],
        head_gain.reshape(1, width),
        ffn_gain.reshape(1, width),
        expert_ids[0].T,
        router_weight[0].T,
        w_gate,
        w_up,
        w_down,
    )
    layer_out = attention + mixture
    return attention.astype(bf16)[None], layer_out.astype(bf16)[None]


def fits_in_vmem(mesh, arrays):
    count = mesh.shape["seq"]
    queries, w_gate = arrays[0], arrays[7]
    tokens, width = queries.shape[1] // count, queries.shape[2]
    held = count * tokens * width * (2 + 4 + 2 + 2) + 12 * width * w_gate.shape[2]
    return held < VMEM_BYTES * 3 // 4


def solution(mesh):
    def layer(*arrays):
        if fits_in_vmem(mesh, arrays):
            body = functools.partial(per_device_ring, arrays[7].shape[0])
        else:
            body = per_device_routed
        return mapped(body)(*arrays)

    def mapped(body):
        return jax.shard_map(
            body,
            mesh=mesh,
            in_specs=(
                P(("groups", "expert"), "seq", None),
                P(("groups", "expert"), "seq", None),
                P(("groups", "expert"), "seq", None),
                P(),
                P(),
                P(("groups", "expert"), "seq", None),
                P(("groups", "expert"), "seq", None),
                P(("seq", "expert"), None, None),
                P(("seq", "expert"), None, None),
                P(("seq", "expert"), None, None),
            ),
            out_specs=(P(("groups", "expert"), "seq", None), P(("groups", "expert"), "seq", None)),
            check_vma=False,
        )

    return layer
```

```python
import functools

import jax
import jax.numpy as jnp
from jax import lax
from jax.experimental import pallas as pl
from jax.experimental.pallas import tpu as pltpu
from jax.sharding import PartitionSpec as P

HEADS = 16
HEAD_DIM = 128


highest = lax.Precision.HIGHEST
epsilon = 1e-06


def prefix(value, axis, join, neutral):
    count, mine = (lax.axis_size(axis), lax.axis_index(axis))
    pieces = lax.all_gather(value, axis)
    subtotal = jnp.full_like(value, 0) + jnp.asarray(neutral, value.dtype)

    def turn(position, subtotal):
        longer = join(subtotal, pieces[position])
        return jnp.where(position < mine, longer, subtotal)

    return lax.fori_loop(0, count - 1, turn, subtotal)


def add_states(earlier, later):
    return earlier + later


def run_expert(inputs, gate_weight, up_weight, down_weight):
    gate_part = jnp.dot(inputs, gate_weight, preferred_element_type=jnp.float32)
    up_part = jnp.dot(inputs, up_weight, preferred_element_type=jnp.float32)
    expert_hidden = (jax.nn.silu(gate_part) * up_part).astype(jnp.bfloat16)
    return jnp.dot(expert_hidden, down_weight, preferred_element_type=jnp.float32).astype(
        jnp.bfloat16
    )


def to_owners(send_slots):
    return lax.all_to_all(send_slots, ("seq", "expert"), split_axis=0, concat_axis=0, tiled=True)


def from_owners(result_slots):
    return lax.all_to_all(result_slots, ("seq", "expert"), split_axis=0, concat_axis=0, tiled=True)


def per_device_routed(
    queries,
    key_rows,
    value_rows,
    head_gain,
    ffn_gain,
    expert_ids,
    router_weight,
    w_gate,
    w_up,
    w_down,
):
    row_count = queries.shape[1]
    model_width = queries.shape[2]
    block_rows = min(row_count, 512)
    block_count = row_count // block_rows
    block_shape = (block_count, block_rows, HEADS, HEAD_DIM)
    query_blocks = queries.reshape(block_shape)
    key_blocks = key_rows.reshape(block_shape)
    value_blocks = value_rows.reshape(block_shape)
    block_states = jnp.einsum(
        "nthd,nthe->nhde", key_blocks, value_blocks, preferred_element_type=jnp.float32
    )
    local_state = jnp.sum(block_states, axis=0)
    carried = prefix(local_state, "seq", add_states, jnp.zeros_like(local_state))
    starts = carried[None] + jnp.cumsum(block_states, axis=0) - block_states
    causal = jnp.arange(block_rows)[:, None] >= jnp.arange(block_rows)[None, :]
    scores = jnp.einsum(
        "nthd,nuhd->nhtu", query_blocks, key_blocks, preferred_element_type=jnp.float32
    )
    scores = jnp.where(causal, scores, 0.0)
    within = jnp.einsum(
        "nhtu,nuhe->nthe", scores, value_blocks.astype(jnp.float32), precision=highest
    )
    before = jnp.einsum(
        "nthd,nhde->nthe", query_blocks.astype(jnp.float32), starts, precision=highest
    )
    heads_raw = (within + before).reshape(row_count, HEADS, HEAD_DIM)
    mean_square = jnp.mean(heads_raw * heads_raw, axis=-1, keepdims=True)
    attention = (
        (heads_raw * lax.rsqrt(mean_square + epsilon)).reshape(row_count, model_width) * head_gain
    ).astype(jnp.bfloat16)
    attn_float = attention.astype(jnp.float32)
    feature_sq = jnp.mean(attn_float * attn_float, axis=-1, keepdims=True)
    normed = (attn_float * lax.rsqrt(feature_sq + epsilon) * ffn_gain).astype(jnp.bfloat16)
    top_count = expert_ids.shape[2]
    owners = lax.axis_size("seq") * lax.axis_size("expert")
    capacity = min(row_count, 3 * row_count * top_count // (2 * owners))
    slot_total = owners * capacity
    route_flat = expert_ids.reshape(row_count * top_count)
    onehot = (route_flat[:, None] == jnp.arange(owners, dtype=jnp.int32)[None, :]).astype(jnp.int32)
    position = jnp.sum(jnp.cumsum(onehot, axis=0) * onehot, axis=1) - 1
    destination = route_flat * capacity + position
    token_order = jnp.arange(row_count * top_count, dtype=jnp.int32) // top_count
    slot_token = jnp.full((slot_total,), row_count, jnp.int32).at[destination].set(token_order)
    send_slots = jnp.take(normed, slot_token, axis=0, mode="fill", fill_value=0).reshape(
        owners, capacity, model_width
    )
    received = to_owners(send_slots).reshape(slot_total, model_width)
    computed = run_expert(received, w_gate[0], w_up[0], w_down[0])
    returned = from_owners(computed.reshape(owners, capacity, model_width)).reshape(
        slot_total, model_width
    )
    picked = jnp.take(returned, destination, axis=0).reshape(row_count, top_count, model_width)
    shares = router_weight[0] / jnp.sum(router_weight[0], axis=-1, keepdims=True)
    mixture = jnp.einsum("tk,tkd->td", shares, picked.astype(jnp.float32), precision=highest)
    layer_out = (attn_float + mixture).astype(jnp.bfloat16)
    return (
        attention.reshape(1, row_count, model_width),
        layer_out.reshape(1, row_count, model_width),
    )


MESH = pl.DeviceIdType.MESH
VMEM_BYTES = 58 * 1024 * 1024
SCAN_PARTS = 8
ROW_PARTS = 4


def layer_kernel(
    count,
    q_hbm, k_hbm, v_hbm, head_gain, ffn_gain, ids_ref, score_ref, wg_ref, wu_ref, wd_ref,
    att_ref, mix_ref,
    q_ref, k_ref, v_ref, w_in, w_out, gates, rows, normed, partial, hidden, share, state, within,
    a_out, a_in, c_out, c_in, b_out, b_in, sum_in, sum_out,
    in_sem, w_sem, w_send, w_recv, gate_send, gate_recv, a_send, a_recv, c_send, c_recv, b_send, b_recv,
    row_send, row_recv, sum_send, sum_recv,
):
    half_ring = count // 2
    group = lax.axis_index("groups")
    me = lax.axis_index("seq")
    core = lax.axis_index("expert")
    z, y = me // 2, me % 2
    ring = jnp.where(y == 0, z, count - 1 - z)

    def at_ring(place):
        place = lax.rem(place + 2 * count, count)
        seq = jnp.where(place < half_ring, 2 * place, 2 * (count - 1 - place) + 1)
        return (group, seq, core)

    right, left = at_ring(ring + 1), at_ring(ring - 1)
    sibling = (group, me, 1 - core)
    tokens, width = q_ref.shape
    low = tokens // 2
    ff = wg_ref.shape[2]
    part = HEADS // SCAN_PARTS

    barrier = pltpu.get_barrier_semaphore()
    for d in range(1, count):
        pl.semaphore_signal(barrier, inc=1, device_id=at_ring(ring + d), device_id_type=MESH)
    pl.semaphore_signal(barrier, inc=1, device_id=sibling, device_id_type=MESH)

    in_copies = [
        pltpu.make_async_copy(k_hbm, k_ref, in_sem.at[0]),
        pltpu.make_async_copy(v_hbm, v_ref, in_sem.at[1]),
        pltpu.make_async_copy(q_hbm, q_ref, in_sem.at[2]),
    ]
    for c in in_copies:
        c.start()
    own_copies = [
        pltpu.make_async_copy(wg_ref.at[0], w_in.at[0], w_sem.at[0]),
        pltpu.make_async_copy(wu_ref.at[0], w_in.at[1], w_sem.at[1]),
        pltpu.make_async_copy(wd_ref.at[0], w_out.at[pl.ds(0, ff)], w_sem.at[2]),
    ]
    for c in own_copies:
        c.start()

    def head(h):
        return pl.ds(h * HEAD_DIM, HEAD_DIM)

    half_rows = HEADS * HEAD_DIM // 2
    piece = half_rows // SCAN_PARTS
    mine, other = y * half_rows, (1 - y) * half_rows

    def head_state(base, h):
        cols = pl.ds(pl.multiple_of(base + h * HEAD_DIM, HEAD_DIM), HEAD_DIM)
        return lax.dot_general(
            k_ref[:, cols], v_ref[:, cols], (((0,), (0,)), ((), ())),
            preferred_element_type=jnp.float32,
        )

    for c in in_copies[:2]:
        c.wait()
    for h in range(HEADS // 2):
        a_out[head(h), :] = head_state(other, h).astype(jnp.bfloat16)

    pl.semaphore_wait(barrier, count)

    def remote(src, dst, send, recv, where):
        return pltpu.make_async_remote_copy(
            src_ref=src, dst_ref=dst, send_sem=send, recv_sem=recv,
            device_id=where, device_id_type=MESH,
        )

    across = (group, me + 1 - 2 * y, core)
    above = (group, lax.rem(me + 2, count), core)

    def span(j):
        return pl.ds(j * piece, piece)

    def a_copy(j):
        return remote(a_out.at[span(j)], a_in.at[span(j)], a_send.at[j], a_recv.at[j], across)

    def b_copy(j):
        return remote(b_out.at[span(j)], b_in.at[span(j)], b_send.at[j], b_recv.at[j], across)

    def c_copy(j):
        return remote(c_out.at[span(j)], c_in.at[span(j)], c_send.at[j], c_recv.at[j], above)

    for j in range(SCAN_PARTS):
        a_copy(j).start()
    for h in range(HEADS // 2):
        state[head(h), :] = head_state(mine, h)
    in_copies[2].wait()

    gate_rows = gates.shape[2] - 8
    picks = lax.broadcasted_iota(jnp.int32, (gate_rows, tokens), 0)
    scores = score_ref[...]
    named = scores / jnp.sum(scores, axis=0, keepdims=True)
    ids = ids_ref[...]
    dense = jnp.zeros((gate_rows, tokens), jnp.float32)
    for t in range(ids.shape[0]):
        dense += jnp.where(ids[t : t + 1, :] == picks, named[t : t + 1, :], 0.0)
    gates[0, 0, pl.ds(0, gate_rows), :] = dense

    causal = lax.broadcasted_iota(jnp.int32, (tokens, tokens), 0) >= lax.broadcasted_iota(
        jnp.int32, (tokens, tokens), 1
    )
    for h in range(HEADS):
        pair = lax.dot_general(
            q_ref[:, head(h)], k_ref[:, head(h)], (((1,), (1,)), ((), ())),
            preferred_element_type=jnp.float32,
        )
        pair = jnp.where(causal, pair, 0.0).astype(jnp.bfloat16)
        within[:, head(h)] = jnp.dot(pair, v_ref[:, head(h)], preferred_element_type=jnp.float32)

    weight_copies = [
        remote(wg_ref.at[0], w_in.at[2], w_send.at[0], w_recv.at[0], sibling),
        remote(wu_ref.at[0], w_in.at[3], w_send.at[1], w_recv.at[1], sibling),
        remote(wd_ref.at[0], w_out.at[pl.ds(ff, ff)], w_send.at[2], w_recv.at[2], sibling),
    ]

    part_width = width // ROW_PARTS

    def row_copy(side, step, i, origin):
        place = lax.rem(origin + 2 * count, count)
        first = jnp.where(place < half_ring, 0, ROW_PARTS // 2)
        c = lax.rem(first + i, ROW_PARTS)
        cols = pl.ds(pl.multiple_of(c * part_width, part_width), part_width)
        src = rows.at[step - 1, pl.ds(0 if step == 1 else side * tokens, tokens), cols]
        if step < half_ring:
            dst = rows.at[step, pl.ds(side * tokens, tokens), cols]
        else:
            dst = rows.at[0, pl.ds(tokens, tokens), cols]
        return remote(
            src, dst, row_send.at[side, step - 1, i], row_recv.at[side, step - 1, i],
            right if side == 0 else left,
        )

    def row_out(side, step, i):
        back = step - 1
        return row_copy(side, step, i, ring - back if side == 0 else ring + back)

    def row_arrival(side, step, i):
        return row_copy(side, step, i, ring - step if side == 0 else ring + step)

    def goes(side, step, i):
        return step < half_ring or (i < ROW_PARTS // 2) == (side == 0)

    def chain(j):
        a_copy(j).wait_recv()

        @pl.when(z == 0)
        def _():
            c_in[span(j), :] = jnp.zeros((piece, HEAD_DIM), jnp.bfloat16)

        @pl.when(z > 0)
        def _():
            c_copy(j).wait_recv()

        earlier = c_in[span(j), :].astype(jnp.float32)
        own = state[span(j), :]
        c_out[span(j), :] = (
            earlier + (own + a_in[span(j), :].astype(jnp.float32))
        ).astype(jnp.bfloat16)

        @pl.when(z < half_ring - 1)
        def _():
            c_copy(j).start()

        b_out[span(j), :] = (earlier + jnp.where(y == 0, own, 0.0)).astype(jnp.bfloat16)
        b_copy(j).start()

    heads_each = piece // HEAD_DIM

    def attend(j):
        if j < SCAN_PARTS:
            base, k = mine, j
            start = c_in[span(k), :].astype(jnp.float32) + jnp.where(
                y == 1, a_in[span(k), :].astype(jnp.float32), 0.0
            )
            start = start.astype(jnp.bfloat16)
        else:
            base, k = other, j - SCAN_PARTS
            b_copy(k).wait_recv()
            start = b_in[span(k), :]
        squares = jnp.zeros((tokens, HEAD_DIM), jnp.float32)
        for i in range(heads_each):
            cols = pl.ds(
                pl.multiple_of(base + k * piece + i * HEAD_DIM, HEAD_DIM), HEAD_DIM
            )
            raw = within[:, cols] + jnp.dot(
                q_ref[:, cols], start[i * HEAD_DIM : (i + 1) * HEAD_DIM],
                preferred_element_type=jnp.float32,
            )
            mean_square = jnp.mean(raw * raw, axis=-1, keepdims=True)
            att = (raw * lax.rsqrt(mean_square + epsilon) * head_gain[:, cols]).astype(
                jnp.bfloat16
            )
            rows[0, pl.ds(0, tokens), cols] = att
            att = att.astype(jnp.float32)
            att_ref[:, cols] = att
            squares += att * att
        each = 2 * SCAN_PARTS // ROW_PARTS
        if (j + 1) % each == 0:
            for side in range(2):
                row_out(side, 1, j // each).start()
        return squares

    square = jnp.zeros((tokens, HEAD_DIM), jnp.float32)
    for j in range(SCAN_PARTS):
        chain(j)
        if j % 2 == 1 and j > 2:
            square += attend(j - 3) + attend(j - 2)
    for j in range(SCAN_PARTS - 2, 2 * SCAN_PARTS):
        square += attend(j)
        if j - SCAN_PARTS + 2 < len(weight_copies):
            weight_copies[j - SCAN_PARTS + 2].start()

    scale = lax.rsqrt(jnp.sum(jnp.transpose(square), axis=0, keepdims=True) / width + epsilon)
    gates[0, 0, pl.ds(gate_rows, 8), :] = jnp.broadcast_to(scale, (8, tokens))
    gate_copies = {}
    for d in range(1, count):
        slot = (d, 0) if d < half_ring else ((0, 1) if d == half_ring else (count - d, 1))
        gate_copies[slot] = remote(
            gates.at[0, 0], gates.at[slot[0], slot[1]],
            gate_send.at[slot[0], slot[1]], gate_recv.at[slot[0], slot[1]],
            at_ring(ring + d),
        )
        gate_copies[slot].start()

    def row_span(side, h):
        return pl.ds(side * tokens + h * low, low)

    line = lax.broadcasted_iota(jnp.int32, (gate_rows + 8, 128), 0)
    lane = lax.broadcasted_iota(jnp.int32, (gate_rows + 8, 128), 1)
    wanted = jnp.where(lane == 0, 2 * me + core, jnp.where(lane == 1, 2 * me + 1 - core, gate_rows))
    chosen = ((line == wanted) & (lane < 3)).astype(jnp.float32)

    def expert_pieces(index, first, size):
        here = pl.ds(first, size)

        def norm():
            for side in range(first // tokens, (first + size) // tokens):
                if (index, side) != (0, 0):
                    gate_copies[(index, side)].wait_recv()
                share[index, pl.ds(side * tokens, tokens), :] = lax.dot_general(
                    gates[index, side], chosen, (((0,), (0,)), ((), ())),
                    preferred_element_type=jnp.float32, precision=highest,
                )
            scale = share[index, here, 2:3]
            for h in range(HEADS):
                normed[here, head(h)] = (
                    rows[index, here, head(h)].astype(jnp.float32) * scale * ffn_gain[:, head(h)]
                ).astype(jnp.bfloat16)

        def into_hidden(e):
            x = normed[here, :]
            gate_part = jnp.dot(x, w_in[2 * e], preferred_element_type=jnp.float32)
            up_part = jnp.dot(x, w_in[2 * e + 1], preferred_element_type=jnp.float32)
            act = gate_part / (1.0 + jnp.exp(-gate_part)) * up_part
            hidden[here, pl.ds(e * ff, ff)] = (
                act * share[index, here, e : e + 1]
            ).astype(jnp.bfloat16)

        def from_hidden():
            partial[index, here, :] = jnp.dot(
                hidden[here, :], w_out[...], preferred_element_type=jnp.float32
            )

        return [
            norm,
            functools.partial(into_hidden, 0),
            functools.partial(into_hidden, 1),
            from_hidden,
        ]

    def sum_copy(side, step, h):
        here = (side, step - 1, pl.ds(h * low, low))
        return remote(
            sum_out.at[here], sum_in.at[here],
            sum_send.at[side, step - 1, h], sum_recv.at[side, step - 1, h],
            right if side == 0 else left,
        )

    def sum_step(side, step, h):
        index = half_ring - step + 1 if step > 1 else 0
        value = partial[index, row_span(1 if step == 1 else 1 - side, h), :]
        if step > 2 or (step == 2 and h == side):
            sum_copy(side, step - 1, h).wait_recv()
            value += sum_in[side, step - 2, pl.ds(h * low, low), :].astype(jnp.float32)
        sum_out[side, step - 1, pl.ds(h * low, low), :] = value.astype(jnp.bfloat16)
        sum_copy(side, step, h).start()

    def take(step, i):
        for side in range(2):
            if goes(side, step, i):
                row_arrival(side, step, i).wait_recv()
            if step < half_ring and goes(side, step + 1, i):
                row_out(side, step + 1, i).start()

    def arrive(i):
        if i == 1:
            own_copies[0].wait()
            own_copies[1].wait()
        if i == 2:
            weight_copies[0].wait_recv()
            weight_copies[1].wait_recv()
        if i == 3:
            own_copies[2].wait()
            weight_copies[2].wait_recv()

    for i in range(ROW_PARTS):
        take(1, i)
    for step in range(1, half_ring):
        for i, work in enumerate(expert_pieces(step, 0, 2 * tokens)):
            if step == 1:
                arrive(i)
            work()
            if step + 1 < half_ring:
                take(step + 1, i)
    for side in range(2):
        sum_step(side, 2, 1 - side)
    for i in range(ROW_PARTS):
        take(half_ring, i)
    for work in expert_pieces(0, tokens, tokens):
        work()
    for side in range(2):
        sum_step(side, 1, side)
    later = []
    for step in range(3, half_ring + 1):
        later += [(step, 0), (step - 1, 1)]
    later.append((half_ring, 1))
    own_work = expert_pieces(0, 0, tokens)
    for step, first in later:
        for side in range(2):
            sum_step(side, step, (1 - side + first) % 2)
        if own_work:
            own_work.pop(0)()
    for work in own_work:
        work()
    for h in range(2):
        total = partial[0, row_span(0, h), :]
        for side in range(2):
            sum_copy(side, half_ring, h).wait_recv()
            total += sum_in[side, half_ring - 1, pl.ds(h * low, low), :].astype(jnp.float32)
        mix_ref[pl.ds(h * low, low), :] = total

    for c in weight_copies + list(gate_copies.values()):
        c.wait_send()
    for j in range(SCAN_PARTS):
        @pl.when(z < half_ring - 1)
        def _():
            c_copy(j).wait_send()

        a_copy(j).wait_send()
        b_copy(j).wait_send()
    for side in range(2):
        for step in range(1, half_ring + 1):
            for i in range(ROW_PARTS):
                if goes(side, step, i):
                    row_out(side, step, i).wait_send()
            for h in range(2):
                if step > 1 or h == side:
                    sum_copy(side, step, h).wait_send()


def per_device_ring(
    experts,
    queries,
    key_rows,
    value_rows,
    head_gain,
    ffn_gain,
    expert_ids,
    router_weight,
    w_gate,
    w_up,
    w_down,
):
    count = lax.axis_size("seq")
    half_ring = count // 2
    tokens, width = queries.shape[1:]
    ff = w_gate.shape[2]
    bf16, f32 = jnp.bfloat16, jnp.float32
    vmem = pl.BlockSpec(memory_space=pltpu.VMEM)
    hbm = pl.BlockSpec(memory_space=pl.ANY)
    dma = pltpu.SemaphoreType.DMA
    half_states = (HEADS * HEAD_DIM // 2, HEAD_DIM)
    gate_rows = -(-experts // 8) * 8 + 8
    attention, mixture = pl.pallas_call(
        functools.partial(layer_kernel, count),
        out_shape=[jax.ShapeDtypeStruct((tokens, width), f32)] * 2,
        in_specs=[hbm] * 3 + [vmem] * 4 + [hbm] * 3,
        out_specs=[vmem] * 2,
        scratch_shapes=[
            pltpu.VMEM((tokens, width), bf16),
            pltpu.VMEM((tokens, width), bf16),
            pltpu.VMEM((tokens, width), bf16),
            pltpu.VMEM((4, width, ff), bf16),
            pltpu.VMEM((2 * ff, width), bf16),
            pltpu.VMEM((half_ring, 2, gate_rows, tokens), f32),
            pltpu.VMEM((half_ring, 2 * tokens, width), bf16),
            pltpu.VMEM((2 * tokens, width), bf16),
            pltpu.VMEM((half_ring, 2 * tokens, width), f32),
            pltpu.VMEM((2 * tokens, 2 * ff), bf16),
            pltpu.VMEM((half_ring, 2 * tokens, 128), f32),
            pltpu.VMEM(half_states, f32),
            pltpu.VMEM((tokens, width), f32),
            pltpu.VMEM(half_states, bf16),
            pltpu.VMEM(half_states, bf16),
            pltpu.VMEM(half_states, bf16),
            pltpu.VMEM(half_states, bf16),
            pltpu.VMEM(half_states, bf16),
            pltpu.VMEM(half_states, bf16),
            pltpu.VMEM((2, half_ring, tokens, width), bf16),
            pltpu.VMEM((2, half_ring, tokens, width), bf16),
            dma((3,)),
            dma((3,)),
            dma((3,)),
            dma((3,)),
            dma((half_ring, 2)),
            dma((half_ring, 2)),
            dma((SCAN_PARTS,)),
            dma((SCAN_PARTS,)),
            dma((SCAN_PARTS,)),
            dma((SCAN_PARTS,)),
            dma((SCAN_PARTS,)),
            dma((SCAN_PARTS,)),
            dma((2, half_ring, ROW_PARTS)),
            dma((2, half_ring, ROW_PARTS)),
            dma((2, half_ring, 2)),
            dma((2, half_ring, 2)),
        ],
        compiler_params=pltpu.CompilerParams(
            collective_id=0, has_side_effects=True, vmem_limit_bytes=VMEM_BYTES
        ),
        cost_estimate=pl.CostEstimate(
            flops=12 * count * tokens * width * ff,
            bytes_accessed=6 * width * ff + 10 * tokens * width,
            transcendentals=2 * count * tokens * ff,
        ),
    )(
        queries[0],
        key_rows[0],
        value_rows[0],
        head_gain.reshape(1, width),
        ffn_gain.reshape(1, width),
        expert_ids[0].T,
        router_weight[0].T,
        w_gate,
        w_up,
        w_down,
    )
    layer_out = attention + mixture
    return attention.astype(bf16)[None], layer_out.astype(bf16)[None]


def fits_in_vmem(mesh, arrays):
    count = mesh.shape["seq"]
    queries, w_gate = arrays[0], arrays[7]
    tokens, width = queries.shape[1] // count, queries.shape[2]
    held = count * tokens * width * (2 + 4 + 2 + 2) + 12 * width * w_gate.shape[2]
    return held < VMEM_BYTES * 3 // 4


def solution(mesh):
    def layer(*arrays):
        if fits_in_vmem(mesh, arrays):
            body = functools.partial(per_device_ring, arrays[7].shape[0])
        else:
            body = per_device_routed
        return mapped(body)(*arrays)

    def mapped(body):
        return jax.shard_map(
            body,
            mesh=mesh,
            in_specs=(
                P(("groups", "expert"), "seq", None),
                P(("groups", "expert"), "seq", None),
                P(("groups", "expert"), "seq", None),
                P(),
                P(),
                P(("groups", "expert"), "seq", None),
                P(("groups", "expert"), "seq", None),
                P(("seq", "expert"), None, None),
                P(("seq", "expert"), None, None),
                P(("seq", "expert"), None, None),
            ),
            out_specs=(P(("groups", "expert"), "seq", None), P(("groups", "expert"), "seq", None)),
            check_vma=False,
        )

    return layer
```
